512 devices in a mesh: dp: 8 (over z_lo, core), expert: 64 (over x, z_hi, y).
Axes of the slice: x: 4, y: 4, z: 16 (z_hi: 4, z_lo: 4; z = z_hi * 4 + z_lo), core: 2. Of those that a mesh axis runs over, the one named last changes fastest.
Arguments:
- grad_out: bfloat16 [16384, 2048], P(('dp', 'expert')), may hold values from -6 to 6
- hidden: bfloat16 [16384, 8, 768], P(('dp', 'expert')), may hold values from -0.29882812 to 0.29882812
- gates: bfloat16 [16384, 8], P(('dp', 'expert')), may hold values from 0.049804688 to 1
- routes: int32 [16384, 8], P(('dp', 'expert')), may hold values from 0 to 63, as said below
- weights: bfloat16 [64, 768, 2048], P('expert'), may hold values from -0.125 to 0.125
Outputs:
- hidden_grad: bfloat16 [16384, 8, 768], P(('dp', 'expert'))
- gate_grad: float32 [16384, 8], P(('dp', 'expert'))
- weight_grad: float32 [64, 768, 2048], P('expert', 'dp')
The draws below stay inside these ranges and needn't reach their ends.
Inputs may be any that keep to these rules, and one draw needn't show every extreme that they name: `routes`: each row names 8 different experts. In each aligned block of 32 rows (the rows of one device) no expert is named more than 12 times, and some expert is named exactly 12 times in every block.
All inputs are finite; a program needn't handle non-finite values.
Results may differ from the reference program's by a relative error of at most 0.015.
Values may be sent and summed in bfloat16 or wider, within the bound.
A program may use at most 128 MiB of HBM per device.

```python
import math
import jax
import jax.numpy as jnp
from jax import lax

D = 2048
F = 768
TOP = 8
TOK_DEV = 32
EXPERTS = 64
TOKENS = 16384
MOST = 12
N_DP = 8


def draw_routes(key, part):
    key = jax.random.fold_in(key, 11)
    per_block = TOK_DEV * TOP
    block_total = TOKENS // TOK_DEV
    cold_total = EXPERTS - 2
    order_key, block_key = jax.random.split(key)
    expert_order = jax.random.permutation(order_key, EXPERTS).astype(jnp.int32)

    def one_block(sub_key):
        second_key, cold_key, token_key, slot_key = jax.random.split(sub_key, 4)
        second = jax.random.randint(second_key, (), (MOST + 1) // 2, MOST + 1).astype(jnp.int32)
        remain = per_block - MOST - second
        base_count = remain // cold_total
        extra_count = remain % cold_total
        cold_rank = jax.random.permutation(cold_key, cold_total).astype(jnp.int32)
        cold_counts = (base_count + (cold_rank < extra_count).astype(jnp.int32)).astype(jnp.int32)
        ordered_counts = jnp.concatenate([jnp.full((1,), MOST, jnp.int32), second[None], cold_counts])
        counts = jnp.zeros((EXPERTS,), jnp.int32).at[expert_order].set(ordered_counts)
        listing = jnp.repeat(jnp.arange(EXPERTS, dtype=jnp.int32), counts, total_repeat_length=per_block)
        route_table = listing.reshape(TOP, TOK_DEV).T
        route_table = route_table[jax.random.permutation(token_key, TOK_DEV)]
        row_keys = jax.random.split(slot_key, TOK_DEV)
        shuffles = jax.vmap(lambda row_key: jax.random.permutation(row_key, TOP))(row_keys)
        return jnp.take_along_axis(route_table, shuffles, axis=1)
    blocks = jax.vmap(one_block)(jax.random.split(block_key, block_total))
    return blocks.reshape(TOKENS, TOP).astype(jnp.int32)


def block_levels(key, shape, cuts, low, largest):
    level, own = 1.0, jax.random.fold_in(key, 6)
    for position, parts in cuts:
        draws = jnp.exp(jax.random.uniform(jax.random.fold_in(own, position), (parts,), jnp.float32, low / len(cuts), largest / len(cuts)))
        level = level * jnp.repeat(draws, shape[position] // parts).reshape([-1 if axis == position else 1 for axis in range(len(shape))])
    return level


def scatter_about(key, dims, spread, most, cuts=(), held_as=jnp.bfloat16):
    factor_of = block_levels(key, dims, cuts, -0.22, 0.18) if cuts else 1.0
    values = jax.random.normal(key, dims, jnp.float32) * spread * factor_of
    return jnp.minimum(jnp.maximum(values, -most), most).astype(held_as)


def setup_inputs(seed: int = 0) -> dict:
    streams_of = jax.random.split(jax.random.key(seed), 6)
    return {
        "grad_out": scatter_about(streams_of[0], (TOKENS, D), 1.0, 6.0, ((0, 512),)),
        "hidden": scatter_about(streams_of[1], (TOKENS, TOP, F), 0.05, 0.29882812, ((0, 512),)),
        "gates": jnp.clip(jnp.exp(math.log(1.0) - 2.9996462 * jax.random.uniform(streams_of[2], (TOKENS, TOP), jnp.float32) ** block_levels(streams_of[2], (TOKENS, TOP), ((0, 512),), -0.2, 0.2)), 0.049804688, 1.0).astype(jnp.bfloat16),
        "routes": draw_routes(jax.random.fold_in(streams_of[5], 71), 0),
        "weights": scatter_about(streams_of[4], (EXPERTS, F, D), D ** -0.5, 0.125, ((0, 64),)),
    }


tile_rows = 128


def replica_part(grad_part, hidden_part, gate_part, route_part, weights):
    token_count, picks_each = route_part.shape
    expert_total, hidden_width, model_width = weights.shape
    route_total = token_count * picks_each
    route_list = route_part.reshape(-1).astype(jnp.int32)
    sorted_routes = jnp.argsort(route_list, stable=True).astype(jnp.int32)
    expert_ids = jnp.arange(expert_total, dtype=jnp.int32)
    counts = jnp.sum((route_list[:, None] == expert_ids[None, :]).astype(jnp.int32), axis=0)
    starts = jnp.cumsum(counts) - counts
    tiles_each = (counts + tile_rows - 1) // tile_rows
    tile_ends = jnp.cumsum(tiles_each)
    tile_begin = tile_ends - tiles_each
    tile_limit = route_total // tile_rows + expert_total
    tile_ids = jnp.arange(tile_limit, dtype=jnp.int32)
    tile_owner = jnp.searchsorted(tile_ends, tile_ids, side="right").astype(jnp.int32)
    owner_safe = jnp.minimum(tile_owner, expert_total - 1).astype(jnp.int32)
    tile_local = tile_ids - tile_begin[owner_safe]
    first_rows = (starts[owner_safe] + tile_local * tile_rows).astype(jnp.int32)
    live_rows = jnp.where(tile_owner < expert_total, counts[owner_safe] - tile_local * tile_rows, 0)
    live_rows = jnp.clip(live_rows, 0, tile_rows).astype(jnp.int32)
    hidden_flat = hidden_part.reshape(route_total, hidden_width)
    gate_flat = gate_part.reshape(-1).astype(jnp.float32)
    row_offsets = jnp.arange(tile_rows, dtype=jnp.int32)

    def tile_work(grad_acc, expert, first_row, live_count):
        valid_mask = row_offsets < live_count
        positions = jnp.clip(first_row + row_offsets, 0, route_total - 1)
        route_ids = sorted_routes[positions]
        grad_tile = grad_part[route_ids // picks_each]
        hidden_tile = hidden_flat[route_ids]
        gate_tile = jnp.where(valid_mask, gate_flat[route_ids], jnp.zeros((), jnp.float32))
        projected = lax.dot_general(grad_tile, weights[expert], (((1,), (1,)), ((), ())), preferred_element_type=jnp.float32).astype(jnp.bfloat16)
        scaled = (gate_tile[:, None] * grad_tile.astype(jnp.float32)).astype(jnp.bfloat16)
        outer_term = lax.dot_general(hidden_tile, scaled, (((0,), (0,)), ((), ())), preferred_element_type=jnp.float32)
        grad_acc = grad_acc.at[expert].add(outer_term)
        target = jnp.where(valid_mask, route_ids, route_total).astype(jnp.int32)
        return grad_acc, projected, target

    def tile_skip(grad_acc, expert, first_row, live_count):
        return grad_acc, jnp.zeros((tile_rows, hidden_width), jnp.bfloat16), jnp.full((tile_rows,), route_total, jnp.int32)

    def tile_step(grad_acc, tile_info):
        expert, first_row, live_count = tile_info
        grad_acc, projected, target = lax.cond(live_count > 0, tile_work, tile_skip, grad_acc, expert, first_row, live_count)
        return grad_acc, (projected, target)

    grad_start = jnp.zeros((expert_total, hidden_width, model_width), jnp.float32)
    grad_acc, (projs, targets) = lax.scan(tile_step, grad_start, (owner_safe, first_rows, live_rows))
    proj_all = jnp.zeros((route_total + 1, hidden_width), jnp.bfloat16).at[targets.reshape(-1)].set(projs.reshape(-1, hidden_width))[:route_total]
    proj_float = proj_all.astype(jnp.float32)
    hidden_grad = (gate_flat[:, None] * proj_float).astype(jnp.bfloat16).reshape(token_count, picks_each, hidden_width)
    gate_grad = jnp.sum(proj_float * hidden_flat.astype(jnp.float32), axis=1).reshape(token_count, picks_each)
    return hidden_grad, gate_grad, grad_acc


def reference(grad_out, hidden, gates, routes, weights):
    replica_rows = TOK_DEV * EXPERTS
    hidden_list = []
    gate_list = []
    weight_grad = jnp.zeros(weights.shape, jnp.float32)
    for replica in range(N_DP):
        row_lower = replica * replica_rows
        row_upper = row_lower + replica_rows
        replica_hidden, replica_gate, replica_weight = replica_part(grad_out[row_lower:row_upper], hidden[row_lower:row_upper], gates[row_lower:row_upper], routes[row_lower:row_upper], weights)
        hidden_list.append(replica_hidden)
        gate_list.append(replica_gate)
        weight_grad = weight_grad + lax.optimization_barrier(replica_weight.astype(jnp.bfloat16)).astype(jnp.float32)
    return jnp.concatenate(hidden_list, axis=0), jnp.concatenate(gate_list, axis=0), weight_grad
```

```python
import functools

import jax
import jax.numpy as jnp
from jax import lax
from jax.experimental import pallas as pl
from jax.experimental.pallas import tpu as pltpu
from jax.sharding import PartitionSpec as P

MESH = pl.DeviceIdType.MESH
BF = jnp.bfloat16
F32 = jnp.float32
I32 = jnp.int32

TOK = 32
TOP = 8
ROUTES = TOK * TOP
D = 2048
F = 768
CUT = 640
SLOT = 16
PEERS = 32
ROWS = PEERS * SLOT
CH = 16
CR = F // CH
SLAB = 192
SUB = 4
SR = SLAB // SUB


def iota(shape, dim):
    return lax.broadcasted_iota(I32, shape, dim)


def dot(a, b, dims=((1,), (0,))):
    return lax.dot_general(a, b, (dims, ((), ())), preferred_element_type=F32)


def pick(mask):
    return jnp.where(mask, 1.0, 0.0).astype(BF)


def kernel(
    routes_ref, gates_ref, grad_ref, hid_ref, w_ref,
    hg_ref, gg_ref, wg_ref,
    tok, meta, meta_out, pack, got, cell, back, rowsel, colsel, gcol_ref,
    wbuf, g, ht, proj5, part, land_p, land_m, fin_out, fin_in,
    w_sem, meta_s, meta_r, tok_s, tok_r, fwd_s, fwd_r, hid_s, hid_r, ret_s, ret_r,
    rel_s, rel_r, rs_s, rs_rp, rs_rm, fin_s, fin_r,
):
    dp = lax.axis_index("dp")
    ex = lax.axis_index("expert")
    zl, c = dp // 2, dp % 2
    x, zb, y = ex // 16, (ex // 4) % 4, ex % 4
    z = zb * 4 + zl
    side = zb % 2 != c
    home = zb % 2 == c
    up = (z + 1) % 16
    down = (z + 15) % 16

    def plane(j, sign):
        dc, dx, dy = j // 16, (j // 4) % 4, j % 4
        if sign < 0:
            dx, dy = 4 - dx, 4 - dy
        return (zl * 2 + (c + dc) % 2, ((x + dx) % 4) * 16 + zb * 4 + (y + dy) % 4)

    def column(zz):
        return ((zz % 4) * 2 + c, x * 16 + (zz // 4) * 4 + y)

    partner = (zl * 2 + (c + 1) % 2, ex)

    def remote(src, dst, s, r, to):
        return pltpu.make_async_remote_copy(
            src_ref=src, dst_ref=dst, send_sem=s, recv_sem=r, device_id=to, device_id_type=MESH
        )

    def slot_rows(j, n=SLOT):
        return pl.ds(pl.multiple_of(j * n, n), n)

    barrier = pltpu.get_barrier_semaphore()

    def greet(j, carry):
        pl.semaphore_signal(barrier, inc=1, device_id=plane(j, 1), device_id_type=MESH)
        return carry

    lax.fori_loop(1, PEERS, greet, 0)
    pl.semaphore_signal(barrier, inc=1, device_id=column(up), device_id_type=MESH)
    pl.semaphore_signal(barrier, inc=1, device_id=column(down), device_id_type=MESH)

    own_q = zb // 2

    @pl.when(home)
    def _():
        pltpu.make_async_copy(w_ref, wbuf.at[own_q], w_sem).start()

    tok[pl.ds(0, TOK), :] = grad_ref[...]

    routes = routes_ref[...].astype(F32)
    shifted = dot(
        routes.astype(BF), pick(iota((TOK, 512), 1) == (iota((TOK, 512), 0) + (iota((TOK, 512), 1) // 128) * 160))
    )
    for v in range(4):
        meta_out[v] = jnp.concatenate(
            [shifted[:, v * 128 : (v + 1) * 128], jnp.zeros((8, 128), F32)], axis=0
        ).astype(BF)
    meta[0] = meta_out[0]

    pl.semaphore_wait(barrier, PEERS - 1 + 2)

    def send_meta(j, carry):
        remote(meta_out.at[j % 4], meta.at[j], meta_s, meta_r, plane(j, 1)).start()
        return carry

    lax.fori_loop(1, PEERS, send_meta, 0)

    def send_tok(j, carry):
        remote(tok.at[pl.ds(0, TOK)], tok.at[slot_rows(j, TOK)], tok_s, tok_r.at[j], plane(j, 1)).start()
        return carry

    lax.fori_loop(1, 16, send_tok, 0)
    remote(tok.at[pl.ds(0, TOK)], tok.at[pl.ds(16 * TOK, TOK)], tok_s, fwd_r, partner).start()

    def w_rows(i):
        return pl.ds(pl.multiple_of(i * CR, CR), CR)

    def w_copy(q, i, way):
        chunk = i if way == 0 else CH - 1 - i
        return remote(
            wbuf.at[q, w_rows(chunk)], wbuf.at[q, w_rows(chunk)],
            rel_s.at[way, i], rel_r.at[way, i], column(up if way == 0 else down),
        )

    @pl.when(home)
    def _():
        pltpu.make_async_copy(w_ref, wbuf.at[own_q], w_sem).wait()

    for way, edge in ((0, 3), (1, 0)):

        @pl.when(home & (zl == edge))
        def _():
            def start(i, carry):
                w_copy(own_q, i, way).start()
                return carry

            lax.fori_loop(0, CH, start, 0)

    rt = routes.astype(BF)
    widen = pick(iota((TOK, ROUTES), 1) // TOP == iota((TOK, ROUTES), 0))
    keep = iota((TOP, ROUTES), 1) % TOP == iota((TOP, ROUTES), 0)
    route_row = jnp.sum(jnp.where(keep, dot(rt, widen), 0.0), axis=0, keepdims=True)
    gate_row = jnp.sum(jnp.where(keep, dot(gates_ref[...], widen), 0.0), axis=0, keepdims=True)
    member = jnp.zeros((64, TOK), F32)
    for k in range(TOP):
        member += jnp.where(iota((64, TOK), 0) == routes_ref[k : k + 1, :], 1.0, 0.0)
    before = pick(iota((TOK, TOK), 0) < iota((TOK, TOK), 1))
    rank = dot(member.astype(BF), before)
    rank = dot(rank.astype(BF), widen)
    route_int = route_row.astype(I32)
    rank_row = jnp.sum(
        jnp.where(iota((64, ROUTES), 0) == route_int, rank, 0.0), axis=0, keepdims=True
    ).astype(I32)
    xe, ze, ye = route_int >> 4, (route_int >> 2) & 3, route_int & 3
    away = (((ze & 1) + c) & 1) * 16 + ((xe - x) & 3) * 4 + ((ye - y) & 3)
    slot_row = ((ze >> 1) * PEERS + away) * SLOT + rank_row
    diag = iota((ROUTES, ROUTES), 0) == iota((ROUTES, ROUTES), 1)
    slot_col = jnp.sum(jnp.where(diag, slot_row.astype(F32), 0.0), axis=1, keepdims=True).astype(I32)
    gcol = jnp.sum(jnp.where(diag, gate_row, 0.0), axis=1, keepdims=True)
    gcol_ref[...] = jnp.broadcast_to(gcol, (ROUTES, 128))

    at0 = iota((2 * ROWS, ROUTES), 0)
    rowsel[0] = pick(at0 == slot_row)
    for j in range(3):
        rowsel[1 + j] = pick((at0 % SLOT >= 12) & (at0 + (4 * j - 12) == slot_row))

    scaled = (hid_ref[...].astype(F32) * gcol).astype(BF)
    tail = scaled[:, CUT:]

    def packed(cols, extra):
        for q in range(2):
            rows = slice(q * ROWS, (q + 1) * ROWS)
            out = dot(rowsel[0, rows], scaled[:, cols])
            add = [dot(rowsel[1 + j, rows], tail) for j in extra]
            if len(add) == 2:
                out = out + jnp.concatenate(add, axis=1)
            elif len(add) == 1:
                out = out + jnp.concatenate([add[0], jnp.zeros((ROWS, 128), F32)], axis=1)
            pack[q, :, cols] = out.astype(BF)

    packed(slice(0, 256), (0, 1))
    packed(slice(256, 512), (2,))
    packed(slice(512, 640), ())

    def send_hid(j, carry):
        remote(pack.at[:, slot_rows(j)], got.at[:, slot_rows(j)], hid_s, hid_r, plane(j, 1)).start()
        return carry

    lax.fori_loop(1, PEERS, send_hid, 0)
    got[:, :SLOT, :] = pack[:, :SLOT, :]

    at1 = iota((ROUTES, 2 * ROWS), 1)
    colsel[0] = pick(at1 == slot_col)
    for j in range(3):
        colsel[1 + j] = pick((at1 % SLOT >= 12) & (at1 + (4 * j - 12) == slot_col))

    q_up = jnp.where(side, ((zb + 3) % 4) // 2, ((zb + 2) % 4) // 2)
    q_down = jnp.where(side, ((zb + 1) % 4) // 2, ((zb + 2) % 4) // 2)

    lag = jnp.where(side, 0, 4)
    streams = ((0, q_up, zl < 3, lag + zl), (1, q_down, zl > 0, lag + 3 - zl))

    def relay(step):
        for way, q, inner, late in streams:
            i = step - late
            first = i < CH // 2
            here = (i >= 0) & (i < jnp.where(side, CH, CH // 2))

            @pl.when(here)
            def _():
                w_copy(q, i, way).wait_recv()

            @pl.when(here & (inner | (side & first)))
            def _():
                w_copy(q, i, way).start()

    def relay_sent(i):
        first = i < CH // 2
        for way, q, inner, _ in streams:

            @pl.when((side & (inner | first)) | (home & (jnp.logical_not(inner) | first)))
            def _():
                w_copy(q, i, way).wait_send()

    def forward(j):
        remote(tok.at[pl.ds(0, TOK)], tok.at[slot_rows(j, TOK)], tok_s, tok_r.at[j], plane(j, 1)).wait_recv()
        remote(tok.at[slot_rows(j, TOK)], tok.at[slot_rows(j + 16, TOK)], fwd_s, fwd_r, partner).start()

    def early(i, carry):
        relay(i)

        @pl.when(i > 0)
        def _():
            forward(2 * i)

        forward(2 * i + 1)
        return carry

    lax.fori_loop(0, 8, early, 0)

    remote(meta.at[pl.ds(1, PEERS - 1)], meta.at[pl.ds(1, PEERS - 1)], meta_s, meta_r, partner).wait_recv()
    remote(tok.at[pl.ds(0, 16 * TOK)], tok.at[pl.ds(16 * TOK, 16 * TOK)], fwd_s, fwd_r, partner).wait_recv()

    block = pick((iota((256, 256), 0) < iota((256, 256), 1)) & (iota((256, 256), 0) // TOK == iota((256, 256), 1) // TOK))

    def gather(group):
        halves = []
        for half in range(2):
            first = group * 8 + half * 4
            total = meta[first, :TOP].astype(F32)
            for j in range(1, 4):
                total += meta[first + j, :TOP].astype(F32)
            halves.append(total)
        named = jnp.concatenate(halves, axis=1).astype(I32)
        hits = []
        for q in range(2):
            mine = x * 16 + (c + 2 * q) * 4 + y
            hits.append(jnp.sum(jnp.where(named == mine, 1.0, 0.0), axis=0, keepdims=True))
        both = jnp.concatenate(hits + [jnp.zeros((6, 256), F32)], axis=0)
        ranks = dot(both.astype(BF), block).astype(I32)
        sel = []
        for q in range(2):
            to = (iota((1, 256), 1) // TOK) * SLOT + ranks[q : q + 1, :]
            to = jnp.where(hits[q] > 0.5, to, -1)
            sel.append(pick(iota((128, 256), 0) == to))
        sel = jnp.concatenate(sel, axis=0)

        def columns(n, carry):
            cols = pl.ds(pl.multiple_of(n * 512, 512), 512)
            out = dot(sel, tok[group * 256 : (group + 1) * 256, cols]).astype(BF)
            g[0, group * 128 : (group + 1) * 128, cols] = out[:128]
            g[1, group * 128 : (group + 1) * 128, cols] = out[128:]
            return carry

        lax.fori_loop(0, D // 512, columns, 0)

    def turn(q):
        row = iota((ROWS, 128), 0) % SLOT
        last = jnp.zeros((ROWS, 128), F32)
        for j in range(3):
            moved = pltpu.roll(got[q, :, j * 128 : (j + 1) * 128].astype(F32), ROWS - 12 + 4 * j, 0)
            last = jnp.where(row // 4 == j, moved, last)
        for j in range(2):
            ht[q, j * 256 : (j + 1) * 256, :] = got[q, :, j * 256 : (j + 1) * 256].T
        ht[q, 512:640, :] = got[q, :, 512:640].T
        ht[q, 640:768, :] = last.astype(BF).T

    def outer(q):
        def columns(n, carry):
            cols = pl.ds(pl.multiple_of(n * 256, 256), 256)
            part[q, :, cols] = dot(ht[q], g[q, :, cols]).astype(BF)
            return carry

        lax.fori_loop(0, D // 256, columns, 0)

    def wait_hid():
        remote(
            got.at[:, pl.ds(SLOT, ROWS - SLOT)], got.at[:, pl.ds(SLOT, ROWS - SLOT)], hid_s, hid_r, partner
        ).wait_recv()

    pieces = [
        lambda: gather(0), lambda: gather(1), lambda: gather(2), lambda: gather(3),
        lambda: (wait_hid(), turn(0)), lambda: (outer(0), turn(1)), lambda: outer(1),
    ]
    for i in range(8, CH + 3):
        relay(i)
        if i - 8 < len(pieces):
            pieces[i - 8]()

    def mine(zd):
        return (zd // 4) % 2 == c

    def own(zd, k):
        return (zd // 4) // 2, pl.ds(pl.multiple_of((zd % 4) * SLAB + k * SR, SR), SR)

    def sub(k):
        return pl.ds(pl.multiple_of(k * SR, SR), SR)

    def hop(src, way, s, k):
        land, sem, to = (land_p, rs_rp, up) if way == 0 else (land_m, rs_rm, down)
        return remote(src, land.at[s, sub(k)], rs_s.at[way, s, k], sem.at[s, k], column(to))

    targets = ((0, lambda s: (z + 7 - s) % 16, 7), (1, lambda s: (z + 8 + s) % 16, 8))

    def launch(k, carry):
        for way, target, _ in targets:
            zd = target(0)

            @pl.when(mine(zd))
            def _():
                q, rows = own(zd, k)
                hop(part.at[q, rows], way, 0, k).start()

        return carry

    lax.fori_loop(0, SUB, launch, 0)

    def add_step(s):
        def body(k, carry):
            for way, target, count in targets:
                if s >= count:
                    continue
                zd = target(s)
                land = land_p if way == 0 else land_m

                @pl.when(mine(zd))
                def _():
                    q, rows = own(zd, k)
                    hop(land.at[s - 1, sub(k)], way, s - 1, k).wait_recv()
                    land[s - 1, sub(k), :] = (
                        land[s - 1, sub(k), :].astype(F32) + part[q, rows, :].astype(F32)
                    ).astype(BF)
                    hop(land.at[s - 1, sub(k)], way, s, k).start()

            return carry

        lax.fori_loop(0, SUB, body, 0)

    def project(q, tile):
        out = dot(g[q], wbuf[q, tile * 256 : (tile + 1) * 256, :], ((1,), (1,)))
        row = iota((ROWS, 128), 0) % SLOT
        if tile == 2:
            proj5[...] = out[:, 128:]
            cell[q, :, 512:640] = out[:, :128].astype(BF)
            return
        for n in range(2):
            j = tile * 2 + n
            part_out = out[:, n * 128 : (n + 1) * 128]
            if j < 3:
                part_out = jnp.where(row >= 12, pltpu.roll(proj5[...], 12 - 4 * j, 0), part_out)
            cell[q, :, j * 128 : (j + 1) * 128] = part_out.astype(BF)

    def send_back():
        def start(j, carry):
            remote(cell.at[:, slot_rows(j)], back.at[:, slot_rows(j)], ret_s, ret_r, plane(j, -1)).start()
            return carry

        lax.fori_loop(1, PEERS, start, 0)
        back[:, :SLOT, :] = cell[:, :SLOT, :]

    def finish():
        remote(
            back.at[:, pl.ds(SLOT, ROWS - SLOT)], back.at[:, pl.ds(SLOT, ROWS - SLOT)], ret_s, ret_r, partner
        ).wait_recv()
        gate = gcol_ref[:, :1]
        total = jnp.zeros((ROUTES, 1), F32)

        def routed(sel, cols):
            return dot(colsel[sel, :, :ROWS], back[0, :, cols]) + dot(colsel[sel, :, ROWS:], back[1, :, cols])

        for lo, hi in ((0, 256), (256, 512), (512, 640), (640, 768)):
            if lo < CUT:
                out = routed(0, slice(lo, hi))
            else:
                out = sum(routed(1 + j, slice(j * 128, (j + 1) * 128)) for j in range(3))
            hg_ref[:, lo:hi] = (gate * out).astype(BF)
            total += jnp.sum(out * hid_ref[:, lo:hi].astype(F32), axis=1, keepdims=True)
        spread = jnp.where(iota((ROUTES, TOP), 0) % TOP == iota((ROUTES, TOP), 1), total, 0.0)
        gg_ref[...] = jnp.sum(spread.reshape(TOK, TOP, TOP), axis=1)

    add_step(1)
    for tile in (2, 0, 1):
        project(0, tile)
    add_step(2)
    for tile in (2, 0, 1):
        project(1, tile)
    send_back()
    add_step(3)
    add_step(4)
    add_step(5)
    finish()
    add_step(6)
    add_step(7)

    @pl.when(mine(z))
    def _():
        def close(n, carry):
            k = jnp.where(n < 2, 2 * (1 - c) + n, 2 * c + n - 2)
            q, rows = own(z, k)
            hop(land_p.at[6, sub(k)], 0, 6, k).wait_recv()
            hop(land_m.at[7, sub(k)], 1, 7, k).wait_recv()
            out = (
                land_p[6, sub(k), :].astype(F32)
                + land_m[7, sub(k), :].astype(F32)
                + part[q, rows, :].astype(F32)
            )

            @pl.when(n < 2)
            def _():
                fin_out[sub(n % 2), :] = out.astype(BF)
                remote(fin_out.at[sub(n % 2)], fin_in.at[sub(n % 2)], fin_s.at[n % 2], fin_r.at[n % 2], partner).start()

            @pl.when(n >= 2)
            def _():
                wg_ref[sub(n % 2), :] = out

            return carry

        lax.fori_loop(0, SUB, close, 0)

        def sent(n, carry):
            remote(fin_out.at[sub(n)], fin_in.at[sub(n)], fin_s.at[n], fin_r.at[n], partner).wait_send()
            return carry

        lax.fori_loop(0, 2, sent, 0)

    @pl.when(jnp.logical_not(mine(z)))
    def _():
        def close(n, carry):
            remote(fin_out.at[sub(n)], fin_in.at[sub(n)], fin_s.at[n], fin_r.at[n], partner).wait_recv()
            wg_ref[sub(n), :] = fin_in[sub(n), :].astype(F32)
            return carry

        lax.fori_loop(0, 2, close, 0)

    remote(meta.at[pl.ds(1, PEERS - 1)], meta.at[pl.ds(1, PEERS - 1)], meta_s, meta_r, partner).wait_send()
    remote(tok.at[pl.ds(0, 16 * TOK)], tok.at[pl.ds(0, 16 * TOK)], tok_s, fwd_r, partner).wait_send()
    remote(tok.at[pl.ds(TOK, 15 * TOK)], tok.at[pl.ds(TOK, 15 * TOK)], fwd_s, fwd_r, partner).wait_send()
    remote(
        pack.at[:, pl.ds(SLOT, ROWS - SLOT)], got.at[:, pl.ds(SLOT, ROWS - SLOT)], hid_s, hid_r, partner
    ).wait_send()
    remote(
        cell.at[:, pl.ds(SLOT, ROWS - SLOT)], back.at[:, pl.ds(SLOT, ROWS - SLOT)], ret_s, ret_r, partner
    ).wait_send()

    def all_relayed(i, carry):
        relay_sent(i)
        return carry

    lax.fori_loop(0, CH, all_relayed, 0)

    def all_added(k, carry):
        for way, target, count in targets:
            for s in range(count):

                @pl.when(mine(target(s)))
                def _():
                    hop(land_m.at[0, sub(k)], way, s, k).wait_send()

        return carry

    lax.fori_loop(0, SUB, all_added, 0)


def on_device(grad_out, hidden, gates, routes, weights):
    tokens, picks = routes.shape
    vmem = pl.BlockSpec(memory_space=pltpu.VMEM)
    dma = pltpu.SemaphoreType.DMA
    hidden_grad, gate_grad, weight_grad = pl.pallas_call(
        kernel,
        out_shape=(
            jax.ShapeDtypeStruct((ROUTES, F), BF),
            jax.ShapeDtypeStruct((TOK, TOP), F32),
            jax.ShapeDtypeStruct((F // 8, D), F32),
        ),
        in_specs=[vmem, vmem, vmem, vmem, pl.BlockSpec(memory_space=pl.ANY)],
        out_specs=(vmem, vmem, vmem),
        scratch_shapes=[
            pltpu.VMEM((PEERS * TOK, D), BF),
            pltpu.VMEM((PEERS, 16, 128), BF),
            pltpu.VMEM((4, 16, 128), BF),
            pltpu.VMEM((2, ROWS, CUT), BF),
            pltpu.VMEM((2, ROWS, CUT), BF),
            pltpu.VMEM((2, ROWS, CUT), BF),
            pltpu.VMEM((2, ROWS, CUT), BF),
            pltpu.VMEM((4, 2 * ROWS, ROUTES), BF),
            pltpu.VMEM((4, ROUTES, 2 * ROWS), BF),
            pltpu.VMEM((ROUTES, 128), F32),
            pltpu.VMEM((2, F, D), BF),
            pltpu.VMEM((2, ROWS, D), BF),
            pltpu.VMEM((2, F, ROWS), BF),
            pltpu.VMEM((ROWS, 128), F32),
            pltpu.VMEM((2, F, D), BF),
            pltpu.VMEM((7, SLAB, D), BF),
            pltpu.VMEM((8, SLAB, D), BF),
            pltpu.VMEM((F // 8, D), BF),
            pltpu.VMEM((F // 8, D), BF),
            dma, dma, dma, dma, dma((16,)), dma, dma, dma, dma, dma, dma,
            dma((2, CH)), dma((2, CH)), dma((2, 8, SUB)), dma((7, SUB)), dma((8, SUB)),
            dma((2,)), dma((2,)),
        ],
        compiler_params=pltpu.CompilerParams(
            collective_id=0, has_side_effects=True, vmem_limit_bytes=60 * 2**20
        ),
        cost_estimate=pl.CostEstimate(flops=10**10, bytes_accessed=10**7, transcendentals=0),
        name="routed_down_backward",
    )(routes.T, gates.T, grad_out, hidden.reshape(ROUTES, F), weights.reshape(F, D))
    return (
        hidden_grad.reshape(tokens, picks, F),
        gate_grad,
        weight_grad.reshape(1, F // 8, D),
    )


def solution(mesh):
    return jax.shard_map(
        on_device,
        mesh=mesh,
        in_specs=(
            P(("dp", "expert"), None),
            P(("dp", "expert"), None, None),
            P(("dp", "expert"), None),
            P(("dp", "expert"), None),
            P("expert", None, None),
        ),
        out_specs=(
            P(("dp", "expert"), None, None),
            P(("dp", "expert"), None),
            P("expert", "dp", None),
        ),
        check_vma=False,
    )
```

```python
import functools

import jax
import jax.numpy as jnp
from jax import lax
from jax.experimental import pallas as pl
from jax.experimental.pallas import tpu as pltpu
from jax.sharding import PartitionSpec as P

MESH = pl.DeviceIdType.MESH
BF = jnp.bfloat16
F32 = jnp.float32
I32 = jnp.int32

TOK = 32
TOP = 8
ROUTES = TOK * TOP
D = 2048
F = 768
CUT = 640
SLOT = 16
PEERS = 32
ROWS = PEERS * SLOT
CH = 24
CR = F // CH
SLAB = 192
SUB = 6
FIRST = 16
SKEW = 2
STEPS = max(CH + 3 * SKEW, CH // 2 + 7 * SKEW)
AHEAD = 4
SR = SLAB // SUB
HALF = SUB // 2


def iota(shape, dim):
    return lax.broadcasted_iota(I32, shape, dim)


def dot(a, b, dims=((1,), (0,))):
    return lax.dot_general(a, b, (dims, ((), ())), preferred_element_type=F32)


def pick(mask):
    return jnp.where(mask, 1.0, 0.0).astype(BF)


def kernel(
    routes_ref, gates_ref, grad_ref, hid_ref, w_ref,
    hg_ref, gg_ref, wg_ref,
    tok, meta, meta_out, pack, got, cell, back, rowsel, colsel, gcol_ref,
    wbuf, g, ht, proj5, part, land_p, land_m, fin_out, fin_in,
    w_sem, meta_s, meta_r, tok_s, tok_r, fwd_s, fwd_r, hid_s, hid_r, ret_s, ret_r,
    rel_s, rel_r, rs_s, rs_rp, rs_rm, fin_s, fin_r,
):
    dp = lax.axis_index("dp")
    ex = lax.axis_index("expert")
    zl, c = dp // 2, dp % 2
    x, zb, y = ex // 16, (ex // 4) % 4, ex % 4
    z = zb * 4 + zl
    side = zb % 2 != c
    home = zb % 2 == c
    up = (z + 1) % 16
    down = (z + 15) % 16

    def plane(j, sign):
        dc, dx, dy = j // 16, (j // 4) % 4, j % 4
        if sign < 0:
            dx, dy = 4 - dx, 4 - dy
        return (zl * 2 + (c + dc) % 2, ((x + dx) % 4) * 16 + zb * 4 + (y + dy) % 4)

    def column(zz):
        return ((zz % 4) * 2 + c, x * 16 + (zz // 4) * 4 + y)

    partner = (zl * 2 + (c + 1) % 2, ex)

    def remote(src, dst, s, r, to):
        return pltpu.make_async_remote_copy(
            src_ref=src, dst_ref=dst, send_sem=s, recv_sem=r, device_id=to, device_id_type=MESH
        )

    def slot_rows(j, n=SLOT):
        return pl.ds(pl.multiple_of(j * n, n), n)

    barrier = pltpu.get_barrier_semaphore()

    def greet(j, carry):
        pl.semaphore_signal(barrier, inc=1, device_id=plane(j, 1), device_id_type=MESH)
        return carry

    lax.fori_loop(1, PEERS, greet, 0)
    pl.semaphore_signal(barrier, inc=1, device_id=column(up), device_id_type=MESH)
    pl.semaphore_signal(barrier, inc=1, device_id=column(down), device_id_type=MESH)

    own_q = zb // 2

    @pl.when(home)
    def _():
        pltpu.make_async_copy(w_ref, wbuf.at[own_q], w_sem).start()

    tok[pl.ds(0, TOK), :] = grad_ref[...]

    routes = routes_ref[...].astype(F32)
    shifted = dot(
        routes.astype(BF), pick(iota((TOK, 512), 1) == (iota((TOK, 512), 0) + (iota((TOK, 512), 1) // 128) * 160))
    )
    for v in range(4):
        meta_out[v] = jnp.concatenate(
            [shifted[:, v * 128 : (v + 1) * 128], jnp.zeros((8, 128), F32)], axis=0
        ).astype(BF)
    meta[0] = meta_out[0]

    @pl.when(home)
    def _():
        pltpu.make_async_copy(w_ref, wbuf.at[own_q], w_sem).wait()

    pl.semaphore_wait(barrier, PEERS - 1 + 2)

    def w_rows(i):
        return pl.ds(pl.multiple_of(i * CR, CR), CR)

    def w_copy(q, i, way):
        chunk = i if way == 0 else CH - 1 - i
        return remote(
            wbuf.at[q, w_rows(chunk)], wbuf.at[q, w_rows(chunk)],
            rel_s.at[way, i], rel_r.at[way, i], column(up if way == 0 else down),
        )

    for way, edge in ((0, 3), (1, 0)):

        @pl.when(home & (zl == edge))
        def _():
            def start(i, carry):
                w_copy(own_q, i, way).start()
                return carry

            lax.fori_loop(0, AHEAD, start, 0)

    def send_tok(j, carry):
        remote(tok.at[pl.ds(0, TOK)], tok.at[slot_rows(j, TOK)], tok_s, tok_r.at[j], plane(j, 1)).start()
        return carry

    lax.fori_loop(1, 16, send_tok, 0)
    remote(tok.at[pl.ds(0, TOK)], tok.at[pl.ds(16 * TOK, TOK)], tok_s, fwd_r, partner).start()

    def send_meta(j, carry):
        remote(meta_out.at[j % 4], meta.at[j], meta_s, meta_r, plane(j, 1)).start()
        return carry

    lax.fori_loop(1, PEERS, send_meta, 0)

    rt = routes.astype(BF)
    widen = pick(iota((TOK, ROUTES), 1) // TOP == iota((TOK, ROUTES), 0))
    keep = iota((TOP, ROUTES), 1) % TOP == iota((TOP, ROUTES), 0)
    route_row = jnp.sum(jnp.where(keep, dot(rt, widen), 0.0), axis=0, keepdims=True)
    gate_row = jnp.sum(jnp.where(keep, dot(gates_ref[...], widen), 0.0), axis=0, keepdims=True)
    member = jnp.zeros((64, TOK), F32)
    for k in range(TOP):
        member += jnp.where(iota((64, TOK), 0) == routes_ref[k : k + 1, :], 1.0, 0.0)
    before = pick(iota((TOK, TOK), 0) < iota((TOK, TOK), 1))
    rank = dot(member.astype(BF), before)
    rank = dot(rank.astype(BF), widen)
    route_int = route_row.astype(I32)
    rank_row = jnp.sum(
        jnp.where(iota((64, ROUTES), 0) == route_int, rank, 0.0), axis=0, keepdims=True
    ).astype(I32)
    xe, ze, ye = route_int >> 4, (route_int >> 2) & 3, route_int & 3
    away = (((ze & 1) + c) & 1) * 16 + ((xe - x) & 3) * 4 + ((ye - y) & 3)
    slot_row = ((ze >> 1) * PEERS + away) * SLOT + rank_row
    diag = iota((ROUTES, ROUTES), 0) == iota((ROUTES, ROUTES), 1)
    slot_col = jnp.sum(jnp.where(diag, slot_row.astype(F32), 0.0), axis=1, keepdims=True).astype(I32)
    gcol = jnp.sum(jnp.where(diag, gate_row, 0.0), axis=1, keepdims=True)
    gcol_ref[...] = jnp.broadcast_to(gcol, (ROUTES, 128))

    at0 = iota((2 * ROWS, ROUTES), 0)
    rowsel[0] = pick(at0 == slot_row)
    for j in range(3):
        rowsel[1 + j] = pick((at0 % SLOT >= 12) & (at0 + (4 * j - 12) == slot_row))

    scaled = (hid_ref[...].astype(F32) * gcol).astype(BF)
    tail = scaled[:, CUT:]

    def packed(cols, extra):
        for q in range(2):
            rows = slice(q * ROWS, (q + 1) * ROWS)
            out = dot(rowsel[0, rows], scaled[:, cols])
            add = [dot(rowsel[1 + j, rows], tail) for j in extra]
            if len(add) == 2:
                out = out + jnp.concatenate(add, axis=1)
            elif len(add) == 1:
                out = out + jnp.concatenate([add[0], jnp.zeros((ROWS, 128), F32)], axis=1)
            pack[q, :, cols] = out.astype(BF)

    packed(slice(0, 256), (0, 1))
    packed(slice(256, 512), (2,))
    packed(slice(512, 640), ())

    def send_hid(j, carry):
        remote(pack.at[:, slot_rows(j)], got.at[:, slot_rows(j)], hid_s, hid_r, plane(j, 1)).start()
        return carry

    lax.fori_loop(1, PEERS, send_hid, 0)
    got[:, :SLOT, :] = pack[:, :SLOT, :]

    at1 = iota((ROUTES, 2 * ROWS), 1)
    colsel[0] = pick(at1 == slot_col)
    for j in range(3):
        colsel[1 + j] = pick((at1 % SLOT >= 12) & (at1 + (4 * j - 12) == slot_col))

    q_up = jnp.where(side, ((zb + 3) % 4) // 2, ((zb + 2) % 4) // 2)
    q_down = jnp.where(side, ((zb + 1) % 4) // 2, ((zb + 2) % 4) // 2)

    lag = jnp.where(side, 0, 4)
    streams = ((0, q_up, zl < 3, SKEW * (lag + zl)), (1, q_down, zl > 0, SKEW * (lag + 3 - zl)))

    def relay(step):
        for way, q, inner, late in streams:
            i = step - late
            first = i < CH // 2
            here = (i >= 0) & (i < jnp.where(side, CH, CH // 2))

            @pl.when(here)
            def _():
                w_copy(q, i, way).wait_recv()

            @pl.when(here & (inner | (side & first)))
            def _():
                w_copy(q, i, way).start()

            @pl.when(home & jnp.logical_not(inner) & (step < CH - AHEAD))
            def _():
                w_copy(own_q, step + AHEAD, way).start()

    def relay_sent(i):
        first = i < CH // 2
        for way, q, inner, _ in streams:

            @pl.when((side & (inner | first)) | (home & (jnp.logical_not(inner) | first)))
            def _():
                w_copy(q, i, way).wait_send()

    def forward(j):
        remote(tok.at[pl.ds(0, TOK)], tok.at[slot_rows(j, TOK)], tok_s, tok_r.at[j], plane(j, 1)).wait_recv()
        remote(tok.at[slot_rows(j, TOK)], tok.at[slot_rows(j + 16, TOK)], fwd_s, fwd_r, partner).start()

    def relay_only(i, carry):
        relay(i)
        return carry

    lax.fori_loop(0, FIRST, relay_only, 0)

    def wait_meta():
        remote(meta.at[pl.ds(1, PEERS - 1)], meta.at[pl.ds(1, PEERS - 1)], meta_s, meta_r, partner).wait_recv()

    def wait_partner():
        remote(tok.at[pl.ds(0, 16 * TOK)], tok.at[pl.ds(16 * TOK, 16 * TOK)], fwd_s, fwd_r, partner).wait_recv()

    def forwards(lo, hi):
        def body(j, carry):
            forward(j)
            return carry

        lax.fori_loop(lo, hi, body, 0)

    block = pick((iota((256, 256), 0) < iota((256, 256), 1)) & (iota((256, 256), 0) // TOK == iota((256, 256), 1) // TOK))

    def gather(group):
        halves = []
        for half in range(2):
            first = group * 8 + half * 4
            total = meta[first, :TOP].astype(F32)
            for j in range(1, 4):
                total += meta[first + j, :TOP].astype(F32)
            halves.append(total)
        named = jnp.concatenate(halves, axis=1).astype(I32)
        hits = []
        for q in range(2):
            mine = x * 16 + (c + 2 * q) * 4 + y
            hits.append(jnp.sum(jnp.where(named == mine, 1.0, 0.0), axis=0, keepdims=True))
        both = jnp.concatenate(hits + [jnp.zeros((6, 256), F32)], axis=0)
        ranks = dot(both.astype(BF), block).astype(I32)
        sel = []
        for q in range(2):
            to = (iota((1, 256), 1) // TOK) * SLOT + ranks[q : q + 1, :]
            to = jnp.where(hits[q] > 0.5, to, -1)
            sel.append(pick(iota((128, 256), 0) == to))
        sel = jnp.concatenate(sel, axis=0)

        def columns(n, carry):
            cols = pl.ds(pl.multiple_of(n * 512, 512), 512)
            out = dot(sel, tok[group * 256 : (group + 1) * 256, cols]).astype(BF)
            g[0, group * 128 : (group + 1) * 128, cols] = out[:128]
            g[1, group * 128 : (group + 1) * 128, cols] = out[128:]
            return carry

        lax.fori_loop(0, D // 512, columns, 0)

    def turn(q):
        row = iota((ROWS, 128), 0) % SLOT
        last = jnp.zeros((ROWS, 128), F32)
        for j in range(3):
            moved = pltpu.roll(got[q, :, j * 128 : (j + 1) * 128].astype(F32), ROWS - 12 + 4 * j, 0)
            last = jnp.where(row // 4 == j, moved, last)
        for j in range(2):
            ht[q, j * 256 : (j + 1) * 256, :] = got[q, :, j * 256 : (j + 1) * 256].T
        ht[q, 512:640, :] = got[q, :, 512:640].T
        ht[q, 640:768, :] = last.astype(BF).T

    def outer(q):
        def columns(n, carry):
            cols = pl.ds(pl.multiple_of(n * 256, 256), 256)
            part[q, :, cols] = dot(ht[q], g[q, :, cols]).astype(BF)
            return carry

        lax.fori_loop(0, D // 256, columns, 0)

    def wait_hid():
        remote(
            got.at[:, pl.ds(SLOT, ROWS - SLOT)], got.at[:, pl.ds(SLOT, ROWS - SLOT)], hid_s, hid_r, partner
        ).wait_recv()

    pieces = [
        lambda: forwards(1, 8), lambda: forwards(8, 16),
        lambda: (wait_meta(), gather(0)), lambda: gather(1),
        lambda: (wait_hid(), turn(0)), lambda: turn(1),
        lambda: (wait_partner(), gather(2)), lambda: gather(3),
        lambda: outer(0), lambda: outer(1),
    ]
    for i, piece in enumerate(pieces):
        relay(FIRST + i)
        piece()

    def mine(zd):
        return (zd // 4) % 2 == c

    def own(zd, k):
        return (zd // 4) // 2, pl.ds(pl.multiple_of((zd % 4) * SLAB + k * SR, SR), SR)

    def sub(k):
        return pl.ds(pl.multiple_of(k * SR, SR), SR)

    def hop(src, way, s, k):
        land, sem, to = (land_p, rs_rp, up) if way == 0 else (land_m, rs_rm, down)
        return remote(src, land.at[s, sub(k)], rs_s.at[way, s, k], sem.at[s, k], column(to))

    targets = ((0, lambda s: (z + 8 - s) % 16), (1, lambda s: (z + 8 + s) % 16))

    def far(way, k):
        return k >= HALF if way == 0 else k < HALF

    def launch(k, carry):
        for way, target in targets:
            for s in range(2):
                zd = target(s)

                @pl.when(mine(zd) & (far(way, k) if s == 0 else jnp.logical_not(far(way, k))))
                def _():
                    q, rows = own(zd, k)
                    hop(part.at[q, rows], way, s, k).start()

        return carry

    lax.fori_loop(0, SUB, launch, 0)
    lax.fori_loop(FIRST + len(pieces), STEPS, relay_only, 0)

    def add_step(s):
        def body(k, carry):
            for way, target in targets:
                zd = target(s)
                land = land_p if way == 0 else land_m

                @pl.when(mine(zd) & (far(way, k) | (s > 1)))
                def _():
                    q, rows = own(zd, k)
                    hop(land.at[s - 1, sub(k)], way, s - 1, k).wait_recv()
                    land[s - 1, sub(k), :] = (
                        land[s - 1, sub(k), :].astype(F32) + part[q, rows, :].astype(F32)
                    ).astype(BF)
                    hop(land.at[s - 1, sub(k)], way, s, k).start()

            return carry

        lax.fori_loop(0, SUB, body, 0)

    def project(q, tile):
        out = dot(g[q], wbuf[q, tile * 256 : (tile + 1) * 256, :], ((1,), (1,)))
        row = iota((ROWS, 128), 0) % SLOT
        if tile == 2:
            proj5[...] = out[:, 128:]
            cell[q, :, 512:640] = out[:, :128].astype(BF)
            return
        for n in range(2):
            j = tile * 2 + n
            part_out = out[:, n * 128 : (n + 1) * 128]
            if j < 3:
                part_out = jnp.where(row >= 12, pltpu.roll(proj5[...], 12 - 4 * j, 0), part_out)
            cell[q, :, j * 128 : (j + 1) * 128] = part_out.astype(BF)

    def send_back():
        def start(j, carry):
            remote(cell.at[:, slot_rows(j)], back.at[:, slot_rows(j)], ret_s, ret_r, plane(j, -1)).start()
            return carry

        lax.fori_loop(1, PEERS, start, 0)
        back[:, :SLOT, :] = cell[:, :SLOT, :]

    def finish():
        remote(
            back.at[:, pl.ds(SLOT, ROWS - SLOT)], back.at[:, pl.ds(SLOT, ROWS - SLOT)], ret_s, ret_r, partner
        ).wait_recv()
        gate = gcol_ref[:, :1]
        total = jnp.zeros((ROUTES, 1), F32)

        def routed(sel, cols):
            return dot(colsel[sel, :, :ROWS], back[0, :, cols]) + dot(colsel[sel, :, ROWS:], back[1, :, cols])

        for lo, hi in ((0, 256), (256, 512), (512, 640), (640, 768)):
            if lo < CUT:
                out = routed(0, slice(lo, hi))
            else:
                out = sum(routed(1 + j, slice(j * 128, (j + 1) * 128)) for j in range(3))
            hg_ref[:, lo:hi] = (gate * out).astype(BF)
            total += jnp.sum(out * hid_ref[:, lo:hi].astype(F32), axis=1, keepdims=True)
        spread = jnp.where(iota((ROUTES, TOP), 0) % TOP == iota((ROUTES, TOP), 1), total, 0.0)
        gg_ref[...] = jnp.sum(spread.reshape(TOK, TOP, TOP), axis=1)

    add_step(1)
    for tile in (2, 0, 1):
        project(0, tile)
    add_step(2)
    for tile in (2, 0, 1):
        project(1, tile)
    send_back()
    add_step(3)
    add_step(4)
    add_step(5)
    finish()
    add_step(6)
    add_step(7)

    @pl.when(mine(z))
    def _():
        def close(n, carry):
            k = jnp.where(n < HALF, HALF * (1 - c) + n, HALF * c + n - HALF)
            q, rows = own(z, k)
            hop(land_p.at[7, sub(k)], 0, 7, k).wait_recv()
            hop(land_m.at[7, sub(k)], 1, 7, k).wait_recv()
            out = (
                land_p[7, sub(k), :].astype(F32)
                + land_m[7, sub(k), :].astype(F32)
                + part[q, rows, :].astype(F32)
            )

            @pl.when(n < HALF)
            def _():
                fin_out[sub(n % HALF), :] = out.astype(BF)
                remote(fin_out.at[sub(n % HALF)], fin_in.at[sub(n % HALF)], fin_s.at[n % HALF], fin_r.at[n % HALF], partner).start()

            @pl.when(n >= HALF)
            def _():
                wg_ref[sub(n % HALF), :] = out

            return carry

        lax.fori_loop(0, SUB, close, 0)

        def sent(n, carry):
            remote(fin_out.at[sub(n)], fin_in.at[sub(n)], fin_s.at[n], fin_r.at[n], partner).wait_send()
            return carry

        lax.fori_loop(0, HALF, sent, 0)

    @pl.when(jnp.logical_not(mine(z)))
    def _():
        def close(n, carry):
            remote(fin_out.at[sub(n)], fin_in.at[sub(n)], fin_s.at[n], fin_r.at[n], partner).wait_recv()
            wg_ref[sub(n), :] = fin_in[sub(n), :].astype(F32)
            return carry

        lax.fori_loop(0, HALF, close, 0)

    remote(meta.at[pl.ds(1, PEERS - 1)], meta.at[pl.ds(1, PEERS - 1)], meta_s, meta_r, partner).wait_send()
    remote(tok.at[pl.ds(0, 16 * TOK)], tok.at[pl.ds(0, 16 * TOK)], tok_s, fwd_r, partner).wait_send()
    remote(tok.at[pl.ds(TOK, 15 * TOK)], tok.at[pl.ds(TOK, 15 * TOK)], fwd_s, fwd_r, partner).wait_send()
    remote(
        pack.at[:, pl.ds(SLOT, ROWS - SLOT)], got.at[:, pl.ds(SLOT, ROWS - SLOT)], hid_s, hid_r, partner
    ).wait_send()
    remote(
        cell.at[:, pl.ds(SLOT, ROWS - SLOT)], back.at[:, pl.ds(SLOT, ROWS - SLOT)], ret_s, ret_r, partner
    ).wait_send()

    def all_relayed(i, carry):
        relay_sent(i)
        return carry

    lax.fori_loop(0, CH, all_relayed, 0)

    def all_added(k, carry):
        for way, target in targets:
            for s in range(8):

                @pl.when(mine(target(s)) & (far(way, k) | (s > 0)))
                def _():
                    hop(land_m.at[0, sub(k)], way, s, k).wait_send()

        return carry

    lax.fori_loop(0, SUB, all_added, 0)


def on_device(grad_out, hidden, gates, routes, weights):
    tokens, picks = routes.shape
    vmem = pl.BlockSpec(memory_space=pltpu.VMEM)
    dma = pltpu.SemaphoreType.DMA
    hidden_grad, gate_grad, weight_grad = pl.pallas_call(
        kernel,
        out_shape=(
            jax.ShapeDtypeStruct((ROUTES, F), BF),
            jax.ShapeDtypeStruct((TOK, TOP), F32),
            jax.ShapeDtypeStruct((F // 8, D), F32),
        ),
        in_specs=[vmem, vmem, vmem, vmem, pl.BlockSpec(memory_space=pl.ANY)],
        out_specs=(vmem, vmem, vmem),
        scratch_shapes=[
            pltpu.VMEM((PEERS * TOK, D), BF),
            pltpu.VMEM((PEERS, 16, 128), BF),
            pltpu.VMEM((4, 16, 128), BF),
            pltpu.VMEM((2, ROWS, CUT), BF),
            pltpu.VMEM((2, ROWS, CUT), BF),
            pltpu.VMEM((2, ROWS, CUT), BF),
            pltpu.VMEM((2, ROWS, CUT), BF),
            pltpu.VMEM((4, 2 * ROWS, ROUTES), BF),
            pltpu.VMEM((4, ROUTES, 2 * ROWS), BF),
            pltpu.VMEM((ROUTES, 128), F32),
            pltpu.VMEM((2, F, D), BF),
            pltpu.VMEM((2, ROWS, D), BF),
            pltpu.VMEM((2, F, ROWS), BF),
            pltpu.VMEM((ROWS, 128), F32),
            pltpu.VMEM((2, F, D), BF),
            pltpu.VMEM((8, SLAB, D), BF),
            pltpu.VMEM((8, SLAB, D), BF),
            pltpu.VMEM((F // 8, D), BF),
            pltpu.VMEM((F // 8, D), BF),
            dma, dma, dma, dma, dma((16,)), dma, dma, dma, dma, dma, dma,
            dma((2, CH)), dma((2, CH)), dma((2, 8, SUB)), dma((8, SUB)), dma((8, SUB)),
            dma((HALF,)), dma((HALF,)),
        ],
        compiler_params=pltpu.CompilerParams(
            collective_id=0, has_side_effects=True, vmem_limit_bytes=60 * 2**20
        ),
        cost_estimate=pl.CostEstimate(flops=10**10, bytes_accessed=10**7, transcendentals=0),
        name="routed_down_backward",
    )(routes.T, gates.T, grad_out, hidden.reshape(ROUTES, F), weights.reshape(F, D))
    return (
        hidden_grad.reshape(tokens, picks, F),
        gate_grad,
        weight_grad.reshape(1, F // 8, D),
    )


def solution(mesh):
    return jax.shard_map(
        on_device,
        mesh=mesh,
        in_specs=(
            P(("dp", "expert"), None),
            P(("dp", "expert"), None, None),
            P(("dp", "expert"), None),
            P(("dp", "expert"), None),
            P("expert", None, None),
        ),
        out_specs=(
            P(("dp", "expert"), None, None),
            P(("dp", "expert"), None),
            P("expert", "dp", None),
        ),
        check_vma=False,
    )
```

```python
import functools

import jax
import jax.numpy as jnp
from jax import lax
from jax.experimental import pallas as pl
from jax.experimental.pallas import tpu as pltpu
from jax.sharding import PartitionSpec as P

MESH = pl.DeviceIdType.MESH
BF = jnp.bfloat16
F32 = jnp.float32
I32 = jnp.int32

TOK = 32
TOP = 8
ROUTES = TOK * TOP
D = 2048
F = 768
CUT = 640
SLOT = 16
PEERS = 32
ROWS = PEERS * SLOT
CH = 48
CR = F // CH
SLAB = 192
SUB = 6
TURN = 8
FIRST = 32
SKEW = 4
PER = 3
RATE = 1
STEPS = max(CH + 3 * SKEW, CH // 2 + 7 * SKEW)
AHEAD = 8
SR = SLAB // SUB
HALF = SUB // 2


def iota(shape, dim):
    return lax.broadcasted_iota(I32, shape, dim)


def dot(a, b, dims=((1,), (0,))):
    return lax.dot_general(a, b, (dims, ((), ())), preferred_element_type=F32)


def pick(mask):
    return jnp.where(mask, 1.0, 0.0).astype(BF)


def kernel(
    routes_ref, gates_ref, grad_ref, hid_ref, w_ref,
    hg_ref, gg_ref, wg_ref,
    tok, meta, meta_out, pack, got, cell, back, rowsel, colsel, gcol_ref,
    wbuf, g, ht, proj5, part, land_p, land_m, fin_out, fin_in,
    w_sem, meta_s, meta_r, tok_s, tok_r, fwd_s, fwd_r, hid_s, hid_r, ret_s, ret_r,
    rel_s, rel_r, rs_s, rs_rp, rs_rm, fin_s, fin_r,
):
    dp = lax.axis_index("dp")
    ex = lax.axis_index("expert")
    zl, c = dp // 2, dp % 2
    x, zb, y = ex // 16, (ex // 4) % 4, ex % 4
    z = zb * 4 + zl
    side = zb % 2 != c
    home = zb % 2 == c
    up = (z + 1) % 16
    down = (z + 15) % 16

    def plane(j, sign):
        dc, dx, dy = j // 16, (j // 4) % 4, j % 4
        if sign < 0:
            dx, dy = 4 - dx, 4 - dy
        return (zl * 2 + (c + dc) % 2, ((x + dx) % 4) * 16 + zb * 4 + (y + dy) % 4)

    def column(zz):
        return ((zz % 4) * 2 + c, x * 16 + (zz // 4) * 4 + y)

    partner = (zl * 2 + (c + 1) % 2, ex)

    def remote(src, dst, s, r, to):
        return pltpu.make_async_remote_copy(
            src_ref=src, dst_ref=dst, send_sem=s, recv_sem=r, device_id=to, device_id_type=MESH
        )

    def slot_rows(j, n=SLOT):
        return pl.ds(pl.multiple_of(j * n, n), n)

    barrier = pltpu.get_barrier_semaphore()

    pl.semaphore_signal(barrier, inc=1, device_id=column(up), device_id_type=MESH)
    pl.semaphore_signal(barrier, inc=1, device_id=column(down), device_id_type=MESH)

    def greet(j, carry):
        pl.semaphore_signal(barrier, inc=1, device_id=plane(j, 1), device_id_type=MESH)
        return carry

    lax.fori_loop(1, PEERS, greet, 0)

    own_q = zb // 2

    @pl.when(home)
    def _():
        pltpu.make_async_copy(w_ref, wbuf.at[own_q], w_sem).start()

    @pl.when(home)
    def _():
        pltpu.make_async_copy(w_ref, wbuf.at[own_q], w_sem).wait()

    pl.semaphore_wait(barrier, PEERS - 1 + 2)

    def w_rows(i):
        return pl.ds(pl.multiple_of(i * CR, CR), CR)

    def w_copy(q, i, way):
        chunk = i if way == 0 else CH - 1 - i
        return remote(
            wbuf.at[q, w_rows(chunk)], wbuf.at[q, w_rows(chunk)],
            rel_s.at[way, i], rel_r.at[way, i], column(up if way == 0 else down),
        )

    for way, edge in ((0, 3), (1, 0)):

        @pl.when(home & (zl == edge))
        def _():
            def start(i, carry):
                w_copy(own_q, i, way).start()
                return carry

            lax.fori_loop(0, AHEAD, start, 0)

    tok[pl.ds(0, TOK), :] = grad_ref[...]

    for j in (4, 12, 1, 3, 8, 2):
        remote(tok.at[pl.ds(0, TOK)], tok.at[pl.ds(j * TOK, TOK)], tok_s, tok_r.at[j], plane(j, 1)).start()
    remote(tok.at[pl.ds(0, TOK)], tok.at[pl.ds(16 * TOK, TOK)], tok_s, fwd_r, partner).start()

    routes = routes_ref[...].astype(F32)
    shifted = dot(
        routes.astype(BF), pick(iota((TOK, 512), 1) == (iota((TOK, 512), 0) + (iota((TOK, 512), 1) // 128) * 160))
    )
    for v in range(4):
        meta_out[v] = jnp.concatenate(
            [shifted[:, v * 128 : (v + 1) * 128], jnp.zeros((8, 128), F32)], axis=0
        ).astype(BF)
    meta[0] = meta_out[0]

    def send_meta(j, carry):
        remote(meta_out.at[j % 4], meta.at[j], meta_s, meta_r, plane(j, 1)).start()
        return carry

    lax.fori_loop(1, PEERS, send_meta, 0)

    rt = routes.astype(BF)
    widen = pick(iota((TOK, ROUTES), 1) // TOP == iota((TOK, ROUTES), 0))
    keep = iota((TOP, ROUTES), 1) % TOP == iota((TOP, ROUTES), 0)
    route_row = jnp.sum(jnp.where(keep, dot(rt, widen), 0.0), axis=0, keepdims=True)
    gate_row = jnp.sum(jnp.where(keep, dot(gates_ref[...], widen), 0.0), axis=0, keepdims=True)
    member = jnp.zeros((64, TOK), F32)
    for k in range(TOP):
        member += jnp.where(iota((64, TOK), 0) == routes_ref[k : k + 1, :], 1.0, 0.0)
    before = pick(iota((TOK, TOK), 0) < iota((TOK, TOK), 1))
    rank = dot(member.astype(BF), before)
    rank = dot(rank.astype(BF), widen)
    route_int = route_row.astype(I32)
    rank_row = jnp.sum(
        jnp.where(iota((64, ROUTES), 0) == route_int, rank, 0.0), axis=0, keepdims=True
    ).astype(I32)
    xe, ze, ye = route_int >> 4, (route_int >> 2) & 3, route_int & 3
    away = (((ze & 1) + c) & 1) * 16 + ((xe - x) & 3) * 4 + ((ye - y) & 3)
    slot_row = ((ze >> 1) * PEERS + away) * SLOT + rank_row
    diag = iota((ROUTES, ROUTES), 0) == iota((ROUTES, ROUTES), 1)
    slot_col = jnp.sum(jnp.where(diag, slot_row.astype(F32), 0.0), axis=1, keepdims=True).astype(I32)
    gcol = jnp.sum(jnp.where(diag, gate_row, 0.0), axis=1, keepdims=True)
    gcol_ref[...] = jnp.broadcast_to(gcol, (ROUTES, 128))

    at0 = iota((2 * ROWS, ROUTES), 0)
    rowsel[0] = pick(at0 == slot_row)
    for j in range(3):
        rowsel[1 + j] = pick((at0 % SLOT >= 12) & (at0 + (4 * j - 12) == slot_row))

    scaled = (hid_ref[...].astype(F32) * gcol).astype(BF)
    tail = scaled[:, CUT:]

    def packed(cols, extra):
        for q in range(2):
            rows = slice(q * ROWS, (q + 1) * ROWS)
            out = dot(rowsel[0, rows], scaled[:, cols])
            add = [dot(rowsel[1 + j, rows], tail) for j in extra]
            if len(add) == 2:
                out = out + jnp.concatenate(add, axis=1)
            elif len(add) == 1:
                out = out + jnp.concatenate([add[0], jnp.zeros((ROWS, 128), F32)], axis=1)
            pack[q, :, cols] = out.astype(BF)

    packed(slice(0, 256), (0, 1))
    packed(slice(256, 512), (2,))
    packed(slice(512, 640), ())

    def send_hid(j, carry):
        remote(pack.at[:, slot_rows(j)], got.at[:, slot_rows(j)], hid_s, hid_r, plane(j, 1)).start()
        return carry

    lax.fori_loop(1, PEERS, send_hid, 0)
    got[:, :SLOT, :] = pack[:, :SLOT, :]

    at1 = iota((ROUTES, 2 * ROWS), 1)
    colsel[0] = pick(at1 == slot_col)
    for j in range(3):
        colsel[1 + j] = pick((at1 % SLOT >= 12) & (at1 + (4 * j - 12) == slot_col))

    q_up = jnp.where(side, ((zb + 3) % 4) // 2, ((zb + 2) % 4) // 2)
    q_down = jnp.where(side, ((zb + 1) % 4) // 2, ((zb + 2) % 4) // 2)

    lag = jnp.where(side, 0, 4)
    streams = ((0, q_up, zl < 3, SKEW * (lag + zl)), (1, q_down, zl > 0, SKEW * (lag + 3 - zl)))

    def relay(step):
        for way, q, inner, late in streams:
            i = step - late
            first = i < CH // 2
            here = (i >= 0) & (i < jnp.where(side, CH, CH // 2))

            @pl.when(here)
            def _():
                w_copy(q, i, way).wait_recv()

            @pl.when(here & (inner | (side & first)))
            def _():
                w_copy(q, i, way).start()

            @pl.when(home & jnp.logical_not(inner) & (step < CH - AHEAD))
            def _():
                w_copy(own_q, step + AHEAD, way).start()

    def relay_sent(i):
        first = i < CH // 2
        for way, q, inner, _ in streams:

            @pl.when((side & (inner | first)) | (home & (jnp.logical_not(inner) | first)))
            def _():
                w_copy(q, i, way).wait_send()

    def tok_wait(j):
        remote(tok.at[pl.ds(0, TOK)], tok.at[slot_rows(j, TOK)], tok_s, tok_r.at[j], plane(j, 1)).wait_recv()

    def turn_tokens():
        for n in range(1, 4):
            tok_wait(n)
            tok_wait(4 * n)

        def start(n, carry):
            dx, dy = 1 + n // 3, 1 + n % 3
            j = 4 * dx + dy
            for half, start_at, to in ((0, 4 * dx, dy), (1, dy, 4 * dx)):
                src = pl.ds(pl.multiple_of(start_at * TOK + half * 16, 16), 16)
                dst = pl.ds(pl.multiple_of(j * TOK + half * 16, 16), 16)
                remote(tok.at[src], tok.at[dst], tok_s, tok_r.at[j], plane(to, 1)).start()
            return carry

        lax.fori_loop(0, 9, start, 0)

    def forward(j):
        @pl.when((j > 4) & (j % 4 != 0))
        def _():
            tok_wait(j)

        remote(tok.at[slot_rows(j, TOK)], tok.at[slot_rows(j + 16, TOK)], fwd_s, fwd_r, partner).start()

    def relay_only(i, carry):
        relay(i)
        return carry

    lax.fori_loop(0, TURN, relay_only, 0)
    turn_tokens()
    lax.fori_loop(TURN, FIRST, relay_only, 0)

    def wait_meta():
        remote(meta.at[pl.ds(1, PEERS - 1)], meta.at[pl.ds(1, PEERS - 1)], meta_s, meta_r, partner).wait_recv()

    def wait_partner():
        remote(tok.at[pl.ds(0, 16 * TOK)], tok.at[pl.ds(16 * TOK, 16 * TOK)], fwd_s, fwd_r, partner).wait_recv()

    def forwards(lo, hi):
        def body(j, carry):
            forward(j)
            return carry

        lax.fori_loop(lo, hi, body, 0)

    block = pick((iota((256, 256), 0) < iota((256, 256), 1)) & (iota((256, 256), 0) // TOK == iota((256, 256), 1) // TOK))

    def gather(group):
        halves = []
        for half in range(2):
            first = group * 8 + half * 4
            total = meta[first, :TOP].astype(F32)
            for j in range(1, 4):
                total += meta[first + j, :TOP].astype(F32)
            halves.append(total)
        named = jnp.concatenate(halves, axis=1).astype(I32)
        hits = []
        for q in range(2):
            mine = x * 16 + (c + 2 * q) * 4 + y
            hits.append(jnp.sum(jnp.where(named == mine, 1.0, 0.0), axis=0, keepdims=True))
        both = jnp.concatenate(hits + [jnp.zeros((6, 256), F32)], axis=0)
        ranks = dot(both.astype(BF), block).astype(I32)
        sel = []
        for q in range(2):
            to = (iota((1, 256), 1) // TOK) * SLOT + ranks[q : q + 1, :]
            to = jnp.where(hits[q] > 0.5, to, -1)
            sel.append(pick(iota((128, 256), 0) == to))
        sel = jnp.concatenate(sel, axis=0)

        def columns(n, carry):
            cols = pl.ds(pl.multiple_of(n * 512, 512), 512)
            out = dot(sel, tok[group * 256 : (group + 1) * 256, cols]).astype(BF)
            g[0, group * 128 : (group + 1) * 128, cols] = out[:128]
            g[1, group * 128 : (group + 1) * 128, cols] = out[128:]
            return carry

        lax.fori_loop(0, D // 512, columns, 0)

    def turn(q):
        row = iota((ROWS, 128), 0) % SLOT
        last = jnp.zeros((ROWS, 128), F32)
        for j in range(3):
            moved = pltpu.roll(got[q, :, j * 128 : (j + 1) * 128].astype(F32), ROWS - 12 + 4 * j, 0)
            last = jnp.where(row // 4 == j, moved, last)
        for j in range(2):
            ht[q, j * 256 : (j + 1) * 256, :] = got[q, :, j * 256 : (j + 1) * 256].T
        ht[q, 512:640, :] = got[q, :, 512:640].T
        ht[q, 640:768, :] = last.astype(BF).T

    def outer(q):
        def columns(n, carry):
            cols = pl.ds(pl.multiple_of(n * 256, 256), 256)
            part[q, :, cols] = dot(ht[q], g[q, :, cols]).astype(BF)
            return carry

        lax.fori_loop(0, D // 256, columns, 0)

    def wait_hid():
        remote(
            got.at[:, pl.ds(SLOT, ROWS - SLOT)], got.at[:, pl.ds(SLOT, ROWS - SLOT)], hid_s, hid_r, partner
        ).wait_recv()

    pieces = [
        lambda: forwards(1, 16),
        lambda: (wait_meta(), gather(0), gather(1)),
        lambda: (wait_hid(), turn(0), turn(1)),
        lambda: (wait_partner(), gather(2), gather(3)),
        lambda: outer(0),
        lambda: outer(1),
    ]
    for i, piece in enumerate(pieces):
        for n in range(PER):
            relay(FIRST + i * PER + n)
        piece()

    def mine(zd):
        return (zd // 4) % 2 == c

    def own(zd, k):
        return (zd // 4) // 2, pl.ds(pl.multiple_of((zd % 4) * SLAB + k * SR, SR), SR)

    def sub(k):
        return pl.ds(pl.multiple_of(k * SR, SR), SR)

    def hop(src, way, s, k):
        land, sem, to = (land_p, rs_rp, up) if way == 0 else (land_m, rs_rm, down)
        return remote(src, land.at[s, sub(k)], rs_s.at[way, s, k], sem.at[s, k], column(to))

    targets = ((0, lambda s: (z + 8 - s) % 16), (1, lambda s: (z + 8 + s) % 16))

    def far(way, k):
        return k >= HALF if way == 0 else k < HALF

    def launch(k, carry):
        for way, target in targets:
            for s in range(2):
                zd = target(s)

                @pl.when(mine(zd) & (far(way, k) if s == 0 else jnp.logical_not(far(way, k))))
                def _():
                    q, rows = own(zd, k)
                    hop(part.at[q, rows], way, s, k).start()

        return carry

    lax.fori_loop(0, SUB, launch, 0)
    def add_sub(n):
        s, k = 1 + n // SUB, n % SUB
        for way, target in targets:
            zd = target(s)
            land = land_p if way == 0 else land_m

            @pl.when(mine(zd) & (far(way, k) | (s > 1)))
            def _():
                q, rows = own(zd, k)
                hop(land.at[s - 1, sub(k)], way, s - 1, k).wait_recv()
                land[s - 1, sub(k), :] = (
                    land[s - 1, sub(k), :].astype(F32) + part[q, rows, :].astype(F32)
                ).astype(BF)
                hop(land.at[s - 1, sub(k)], way, s, k).start()

    def adds(lo, hi):
        def body(n, carry):
            add_sub(n)
            return carry

        lax.fori_loop(lo, hi, body, 0)

    last = FIRST + len(pieces) * PER

    def both(i, carry):
        relay(i)
        for r in range(RATE):
            add_sub((i - last) * RATE + r)
        return carry

    lax.fori_loop(last, STEPS, both, 0)
    done = (STEPS - last) * RATE

    def project(q, tile):
        out = dot(g[q], wbuf[q, tile * 256 : (tile + 1) * 256, :], ((1,), (1,)))
        row = iota((ROWS, 128), 0) % SLOT
        if tile == 2:
            proj5[...] = out[:, 128:]
            cell[q, :, 512:640] = out[:, :128].astype(BF)
            return
        for n in range(2):
            j = tile * 2 + n
            part_out = out[:, n * 128 : (n + 1) * 128]
            if j < 3:
                part_out = jnp.where(row >= 12, pltpu.roll(proj5[...], 12 - 4 * j, 0), part_out)
            cell[q, :, j * 128 : (j + 1) * 128] = part_out.astype(BF)

    def send_back():
        def start(j, carry):
            remote(cell.at[:, slot_rows(j)], back.at[:, slot_rows(j)], ret_s, ret_r, plane(j, -1)).start()
            return carry

        lax.fori_loop(1, PEERS, start, 0)
        back[:, :SLOT, :] = cell[:, :SLOT, :]

    def finish():
        remote(
            back.at[:, pl.ds(SLOT, ROWS - SLOT)], back.at[:, pl.ds(SLOT, ROWS - SLOT)], ret_s, ret_r, partner
        ).wait_recv()
        gate = gcol_ref[:, :1]
        total = jnp.zeros((ROUTES, 1), F32)

        def routed(sel, cols):
            return dot(colsel[sel, :, :ROWS], back[0, :, cols]) + dot(colsel[sel, :, ROWS:], back[1, :, cols])

        for lo, hi in ((0, 256), (256, 512), (512, 640), (640, 768)):
            if lo < CUT:
                out = routed(0, slice(lo, hi))
            else:
                out = sum(routed(1 + j, slice(j * 128, (j + 1) * 128)) for j in range(3))
            hg_ref[:, lo:hi] = (gate * out).astype(BF)
            total += jnp.sum(out * hid_ref[:, lo:hi].astype(F32), axis=1, keepdims=True)
        spread = jnp.where(iota((ROUTES, TOK), 0) // TOP == iota((ROUTES, TOK), 1), total, 0.0)
        gg_ref[...] = jnp.sum(spread.reshape(TOK, TOP, TOK), axis=0)

    marks = [done, done + SUB, done + 2 * SUB, 5 * SUB, 7 * SUB]
    adds(marks[0], marks[1])
    for tile in (2, 0, 1):
        project(0, tile)
    adds(marks[1], marks[2])
    for tile in (2, 0, 1):
        project(1, tile)
    send_back()
    adds(marks[2], marks[3])
    finish()
    adds(marks[3], marks[4])

    @pl.when(mine(z))
    def _():
        def close(n, carry):
            k = jnp.where(n < HALF, HALF * (1 - c) + n, HALF * c + n - HALF)
            q, rows = own(z, k)
            hop(land_p.at[7, sub(k)], 0, 7, k).wait_recv()
            hop(land_m.at[7, sub(k)], 1, 7, k).wait_recv()
            out = (
                land_p[7, sub(k), :].astype(F32)
                + land_m[7, sub(k), :].astype(F32)
                + part[q, rows, :].astype(F32)
            )

            @pl.when(n < HALF)
            def _():
                fin_out[sub(n % HALF), :] = out.astype(BF)
                remote(fin_out.at[sub(n % HALF)], fin_in.at[sub(n % HALF)], fin_s.at[n % HALF], fin_r.at[n % HALF], partner).start()

            @pl.when(n >= HALF)
            def _():
                wg_ref[sub(n % HALF), :] = out

            return carry

        lax.fori_loop(0, SUB, close, 0)

        def sent(n, carry):
            remote(fin_out.at[sub(n)], fin_in.at[sub(n)], fin_s.at[n], fin_r.at[n], partner).wait_send()
            return carry

        lax.fori_loop(0, HALF, sent, 0)

    @pl.when(jnp.logical_not(mine(z)))
    def _():
        def close(n, carry):
            remote(fin_out.at[sub(n)], fin_in.at[sub(n)], fin_s.at[n], fin_r.at[n], partner).wait_recv()
            wg_ref[sub(n), :] = fin_in[sub(n), :].astype(F32)
            return carry

        lax.fori_loop(0, HALF, close, 0)

    remote(meta.at[pl.ds(1, PEERS - 1)], meta.at[pl.ds(1, PEERS - 1)], meta_s, meta_r, partner).wait_send()
    remote(tok.at[pl.ds(0, 16 * TOK)], tok.at[pl.ds(0, 16 * TOK)], tok_s, fwd_r, partner).wait_send()
    remote(tok.at[pl.ds(TOK, 15 * TOK)], tok.at[pl.ds(TOK, 15 * TOK)], fwd_s, fwd_r, partner).wait_send()
    remote(
        pack.at[:, pl.ds(SLOT, ROWS - SLOT)], got.at[:, pl.ds(SLOT, ROWS - SLOT)], hid_s, hid_r, partner
    ).wait_send()
    remote(
        cell.at[:, pl.ds(SLOT, ROWS - SLOT)], back.at[:, pl.ds(SLOT, ROWS - SLOT)], ret_s, ret_r, partner
    ).wait_send()

    def all_relayed(i, carry):
        relay_sent(i)
        return carry

    lax.fori_loop(0, CH, all_relayed, 0)

    def all_added(k, carry):
        for way, target in targets:
            for s in range(8):

                @pl.when(mine(target(s)) & (far(way, k) | (s > 0)))
                def _():
                    hop(land_m.at[0, sub(k)], way, s, k).wait_send()

        return carry

    lax.fori_loop(0, SUB, all_added, 0)


def settle(*refs):
    held, sems = refs[6:9], refs[9]
    into = [pltpu.make_async_copy(refs[i], held[i], sems.at[0, i]) for i in range(3)]
    out = [pltpu.make_async_copy(held[i], refs[3 + i], sems.at[1, i]) for i in range(3)]
    for copy in into:
        copy.start()
    for i in range(3):
        into[i].wait()
        out[i].start()
    for copy in out:
        copy.wait()


def on_device(grad_out, hidden, gates, routes, weights):
    tokens, picks = routes.shape
    vmem = pl.BlockSpec(memory_space=pltpu.VMEM)
    dma = pltpu.SemaphoreType.DMA
    results = pl.pallas_call(
        kernel,
        out_shape=(
            jax.ShapeDtypeStruct((ROUTES, F), BF),
            jax.ShapeDtypeStruct((TOP, TOK), F32),
            jax.ShapeDtypeStruct((F // 8, D), F32),
        ),
        in_specs=[vmem, vmem, vmem, vmem, pl.BlockSpec(memory_space=pl.ANY)],
        out_specs=(vmem, vmem, vmem),
        scratch_shapes=[
            pltpu.VMEM((PEERS * TOK, D), BF),
            pltpu.VMEM((PEERS, 16, 128), BF),
            pltpu.VMEM((4, 16, 128), BF),
            pltpu.VMEM((2, ROWS, CUT), BF),
            pltpu.VMEM((2, ROWS, CUT), BF),
            pltpu.VMEM((2, ROWS, CUT), BF),
            pltpu.VMEM((2, ROWS, CUT), BF),
            pltpu.VMEM((4, 2 * ROWS, ROUTES), BF),
            pltpu.VMEM((4, ROUTES, 2 * ROWS), BF),
            pltpu.VMEM((ROUTES, 128), F32),
            pltpu.VMEM((2, F, D), BF),
            pltpu.VMEM((2, ROWS, D), BF),
            pltpu.VMEM((2, F, ROWS), BF),
            pltpu.VMEM((ROWS, 128), F32),
            pltpu.VMEM((2, F, D), BF),
            pltpu.VMEM((8, SLAB, D), BF),
            pltpu.VMEM((8, SLAB, D), BF),
            pltpu.VMEM((F // 8, D), BF),
            pltpu.VMEM((F // 8, D), BF),
            dma, dma, dma, dma, dma((16,)), dma, dma, dma, dma, dma, dma,
            dma((2, CH)), dma((2, CH)), dma((2, 8, SUB)), dma((8, SUB)), dma((8, SUB)),
            dma((HALF,)), dma((HALF,)),
        ],
        compiler_params=pltpu.CompilerParams(
            collective_id=0, has_side_effects=True, vmem_limit_bytes=60 * 2**20
        ),
        cost_estimate=pl.CostEstimate(flops=10**10, bytes_accessed=10**7, transcendentals=0),
        name="routed_down_backward",
    )(routes.T, gates.T, grad_out, hidden.reshape(ROUTES, F), weights.reshape(F, D))
    anywhere = pl.BlockSpec(memory_space=pl.ANY)
    hidden_grad, gate_grad, weight_grad = pl.pallas_call(
        settle,
        out_shape=tuple(jax.ShapeDtypeStruct(r.shape, r.dtype) for r in results),
        in_specs=[anywhere] * 3,
        out_specs=(anywhere,) * 3,
        scratch_shapes=[*(pltpu.VMEM(r.shape, r.dtype) for r in results), dma((2, 3))],
        name="settle_results",
    )(*results)
    return (
        hidden_grad.reshape(tokens, picks, F),
        gate_grad.T,
        weight_grad.reshape(1, F // 8, D),
    )


def solution(mesh):
    return jax.shard_map(
        on_device,
        mesh=mesh,
        in_specs=(
            P(("dp", "expert"), None),
            P(("dp", "expert"), None, None),
            P(("dp", "expert"), None),
            P(("dp", "expert"), None),
            P("expert", None, None),
        ),
        out_specs=(
            P(("dp", "expert"), None, None),
            P(("dp", "expert"), None),
            P("expert", "dp", None),
        ),
        check_vma=False,
    )
```

```python
import functools

import jax
import jax.numpy as jnp
from jax import lax
from jax.experimental import pallas as pl
from jax.experimental.pallas import tpu as pltpu
from jax.sharding import PartitionSpec as P

MESH = pl.DeviceIdType.MESH
BF = jnp.bfloat16
F32 = jnp.float32
I32 = jnp.int32

TOK = 32
TOP = 8
ROUTES = TOK * TOP
D = 2048
F = 768
CUT = 640
SLOT = 16
PEERS = 32
ROWS = PEERS * SLOT
CH = 48
CR = F // CH
SLAB = 192
SUB = 6
TURN = 10
FIRST = 32
SKEW = 4
PER = 3
RATE = 1
STEPS = max(CH + 3 * SKEW, CH // 2 + 7 * SKEW)
AHEAD = 8
SR = SLAB // SUB
HALF = SUB // 2


def iota(shape, dim):
    return lax.broadcasted_iota(I32, shape, dim)


def dot(a, b, dims=((1,), (0,))):
    return lax.dot_general(a, b, (dims, ((), ())), preferred_element_type=F32)


def pick(mask):
    return jnp.where(mask, 1.0, 0.0).astype(BF)


def kernel(
    routes_ref, gates_ref, grad_ref, hid_ref, w_ref,
    hg_ref, gg_ref, wg_ref,
    tok, meta, meta_out, pack, got, cell, back, rowsel, colsel, gcol_ref,
    wbuf, g, ht, proj5, part, land_p, land_m, fin_out, fin_in,
    w_sem, meta_s, meta_r, tok_s, tok_r, fwd_s, fwd_r, hid_s, hid_r, ret_s, ret_r,
    rel_s, rel_r, rs_s, rs_rp, rs_rm, fin_s, fin_r,
):
    dp = lax.axis_index("dp")
    ex = lax.axis_index("expert")
    zl, c = dp // 2, dp % 2
    x, zb, y = ex // 16, (ex // 4) % 4, ex % 4
    z = zb * 4 + zl
    side = zb % 2 != c
    home = zb % 2 == c
    up = (z + 1) % 16
    down = (z + 15) % 16

    def plane(j, sign):
        dc, dx, dy = j // 16, (j // 4) % 4, j % 4
        if sign < 0:
            dx, dy = 4 - dx, 4 - dy
        return (zl * 2 + (c + dc) % 2, ((x + dx) % 4) * 16 + zb * 4 + (y + dy) % 4)

    def column(zz):
        return ((zz % 4) * 2 + c, x * 16 + (zz // 4) * 4 + y)

    partner = (zl * 2 + (c + 1) % 2, ex)

    def remote(src, dst, s, r, to):
        return pltpu.make_async_remote_copy(
            src_ref=src, dst_ref=dst, send_sem=s, recv_sem=r, device_id=to, device_id_type=MESH
        )

    def slot_rows(j, n=SLOT):
        return pl.ds(pl.multiple_of(j * n, n), n)

    barrier = pltpu.get_barrier_semaphore()

    pl.semaphore_signal(barrier, inc=1, device_id=column(up), device_id_type=MESH)
    pl.semaphore_signal(barrier, inc=1, device_id=column(down), device_id_type=MESH)

    def greet(j, carry):
        pl.semaphore_signal(barrier, inc=1, device_id=plane(j, 1), device_id_type=MESH)
        return carry

    lax.fori_loop(1, PEERS, greet, 0)

    own_q = zb // 2

    @pl.when(home)
    def _():
        pltpu.make_async_copy(w_ref, wbuf.at[own_q], w_sem).start()

    @pl.when(home)
    def _():
        pltpu.make_async_copy(w_ref, wbuf.at[own_q], w_sem).wait()

    pl.semaphore_wait(barrier, PEERS - 1 + 2)

    def w_rows(i):
        return pl.ds(pl.multiple_of(i * CR, CR), CR)

    def w_copy(q, i, way):
        chunk = i if way == 0 else CH - 1 - i
        return remote(
            wbuf.at[q, w_rows(chunk)], wbuf.at[q, w_rows(chunk)],
            rel_s.at[way, i], rel_r.at[way, i], column(up if way == 0 else down),
        )

    for way, edge in ((0, 3), (1, 0)):

        @pl.when(home & (zl == edge))
        def _():
            def start(i, carry):
                w_copy(own_q, i, way).start()
                return carry

            lax.fori_loop(0, AHEAD, start, 0)

    tok[pl.ds(0, TOK), :] = grad_ref[...]

    for j in (4, 12, 1, 3, 8, 2):
        remote(tok.at[pl.ds(0, TOK)], tok.at[pl.ds(j * TOK, TOK)], tok_s, tok_r.at[j], plane(j, 1)).start()
    remote(tok.at[pl.ds(0, TOK)], tok.at[pl.ds(16 * TOK, TOK)], tok_s, fwd_r, partner).start()

    routes = routes_ref[...].astype(F32)
    shifted = dot(
        routes.astype(BF), pick(iota((TOK, 512), 1) == (iota((TOK, 512), 0) + (iota((TOK, 512), 1) // 128) * 160))
    )
    for v in range(4):
        meta_out[v] = jnp.concatenate(
            [shifted[:, v * 128 : (v + 1) * 128], jnp.zeros((8, 128), F32)], axis=0
        ).astype(BF)
    meta[0] = meta_out[0]

    def send_meta(j, carry):
        remote(meta_out.at[j % 4], meta.at[j], meta_s, meta_r, plane(j, 1)).start()
        return carry

    lax.fori_loop(1, PEERS, send_meta, 0)

    rt = routes.astype(BF)
    widen = pick(iota((TOK, ROUTES), 1) // TOP == iota((TOK, ROUTES), 0))
    keep = iota((TOP, ROUTES), 1) % TOP == iota((TOP, ROUTES), 0)
    route_row = jnp.sum(jnp.where(keep, dot(rt, widen), 0.0), axis=0, keepdims=True)
    gate_row = jnp.sum(jnp.where(keep, dot(gates_ref[...], widen), 0.0), axis=0, keepdims=True)
    member = jnp.zeros((64, TOK), F32)
    for k in range(TOP):
        member += jnp.where(iota((64, TOK), 0) == routes_ref[k : k + 1, :], 1.0, 0.0)
    before = pick(iota((TOK, TOK), 0) < iota((TOK, TOK), 1))
    rank = dot(member.astype(BF), before)
    rank = dot(rank.astype(BF), widen)
    route_int = route_row.astype(I32)
    rank_row = jnp.sum(
        jnp.where(iota((64, ROUTES), 0) == route_int, rank, 0.0), axis=0, keepdims=True
    ).astype(I32)
    xe, ze, ye = route_int >> 4, (route_int >> 2) & 3, route_int & 3
    away = (((ze & 1) + c) & 1) * 16 + ((xe - x) & 3) * 4 + ((ye - y) & 3)
    slot_row = ((ze >> 1) * PEERS + away) * SLOT + rank_row
    diag = iota((ROUTES, ROUTES), 0) == iota((ROUTES, ROUTES), 1)
    slot_col = jnp.sum(jnp.where(diag, slot_row.astype(F32), 0.0), axis=1, keepdims=True).astype(I32)
    gcol = jnp.sum(jnp.where(diag, gate_row, 0.0), axis=1, keepdims=True)
    gcol_ref[...] = jnp.broadcast_to(gcol, (ROUTES, 128))

    at0 = iota((2 * ROWS, ROUTES), 0)
    rowsel[0] = pick(at0 == slot_row)
    for j in range(3):
        rowsel[1 + j] = pick((at0 % SLOT >= 12) & (at0 + (4 * j - 12) == slot_row))

    scaled = (hid_ref[...].astype(F32) * gcol).astype(BF)
    tail = scaled[:, CUT:]

    def packed(cols, extra):
        for q in range(2):
            rows = slice(q * ROWS, (q + 1) * ROWS)
            out = dot(rowsel[0, rows], scaled[:, cols])
            add = [dot(rowsel[1 + j, rows], tail) for j in extra]
            if len(add) == 2:
                out = out + jnp.concatenate(add, axis=1)
            elif len(add) == 1:
                out = out + jnp.concatenate([add[0], jnp.zeros((ROWS, 128), F32)], axis=1)
            pack[q, :, cols] = out.astype(BF)

    packed(slice(0, 256), (0, 1))
    packed(slice(256, 512), (2,))
    packed(slice(512, 640), ())

    def send_hid(j, carry):
        remote(pack.at[:, slot_rows(j)], got.at[:, slot_rows(j)], hid_s, hid_r, plane(j, 1)).start()
        return carry

    lax.fori_loop(1, PEERS, send_hid, 0)
    got[:, :SLOT, :] = pack[:, :SLOT, :]

    at1 = iota((ROUTES, 2 * ROWS), 1)
    colsel[0] = pick(at1 == slot_col)
    for j in range(3):
        colsel[1 + j] = pick((at1 % SLOT >= 12) & (at1 + (4 * j - 12) == slot_col))

    q_up = jnp.where(side, ((zb + 3) % 4) // 2, ((zb + 2) % 4) // 2)
    q_down = jnp.where(side, ((zb + 1) % 4) // 2, ((zb + 2) % 4) // 2)

    lag = jnp.where(side, 0, 4)
    streams = ((0, q_up, zl < 3, SKEW * (lag + zl)), (1, q_down, zl > 0, SKEW * (lag + 3 - zl)))

    def relay(step):
        for way, q, inner, late in streams:
            i = step - late
            first = i < CH // 2
            here = (i >= 0) & (i < jnp.where(side, CH, CH // 2))

            @pl.when(here)
            def _():
                w_copy(q, i, way).wait_recv()

            @pl.when(here & (inner | (side & first)))
            def _():
                w_copy(q, i, way).start()

            @pl.when(home & jnp.logical_not(inner) & (step < CH - AHEAD))
            def _():
                w_copy(own_q, step + AHEAD, way).start()

    def relay_sent(i):
        first = i < CH // 2
        for way, q, inner, _ in streams:

            @pl.when((side & (inner | first)) | (home & (jnp.logical_not(inner) | first)))
            def _():
                w_copy(q, i, way).wait_send()

    def tok_wait(j):
        remote(tok.at[pl.ds(0, TOK)], tok.at[slot_rows(j, TOK)], tok_s, tok_r.at[j], plane(j, 1)).wait_recv()

    def turn_tokens():
        for n in range(1, 4):
            tok_wait(n)
            tok_wait(4 * n)

        def start(n, carry):
            dx, dy = 1 + n // 3, 1 + n % 3
            j = 4 * dx + dy
            for half, start_at, to in ((0, 4 * dx, dy), (1, dy, 4 * dx)):
                src = pl.ds(pl.multiple_of(start_at * TOK + half * 16, 16), 16)
                dst = pl.ds(pl.multiple_of(j * TOK + half * 16, 16), 16)
                remote(tok.at[src], tok.at[dst], tok_s, tok_r.at[j], plane(to, 1)).start()
            return carry

        lax.fori_loop(0, 9, start, 0)

    def forward(j):
        @pl.when((j > 4) & (j % 4 != 0))
        def _():
            tok_wait(j)

        remote(tok.at[slot_rows(j, TOK)], tok.at[slot_rows(j + 16, TOK)], fwd_s, fwd_r, partner).start()

    def relay_only(i, carry):
        relay(i)
        return carry

    lax.fori_loop(0, TURN, relay_only, 0)
    turn_tokens()
    lax.fori_loop(TURN, FIRST, relay_only, 0)

    def wait_meta():
        remote(meta.at[pl.ds(1, PEERS - 1)], meta.at[pl.ds(1, PEERS - 1)], meta_s, meta_r, partner).wait_recv()

    def wait_partner():
        remote(tok.at[pl.ds(0, 16 * TOK)], tok.at[pl.ds(16 * TOK, 16 * TOK)], fwd_s, fwd_r, partner).wait_recv()

    def forwards(lo, hi):
        def body(j, carry):
            forward(j)
            return carry

        lax.fori_loop(lo, hi, body, 0)

    block = pick((iota((256, 256), 0) < iota((256, 256), 1)) & (iota((256, 256), 0) // TOK == iota((256, 256), 1) // TOK))

    def gather(group):
        halves = []
        for half in range(2):
            first = group * 8 + half * 4
            total = meta[first, :TOP].astype(F32)
            for j in range(1, 4):
                total += meta[first + j, :TOP].astype(F32)
            halves.append(total)
        named = jnp.concatenate(halves, axis=1).astype(I32)
        hits = []
        for q in range(2):
            mine = x * 16 + (c + 2 * q) * 4 + y
            hits.append(jnp.sum(jnp.where(named == mine, 1.0, 0.0), axis=0, keepdims=True))
        both = jnp.concatenate(hits + [jnp.zeros((6, 256), F32)], axis=0)
        ranks = dot(both.astype(BF), block).astype(I32)
        sel = []
        for q in range(2):
            to = (iota((1, 256), 1) // TOK) * SLOT + ranks[q : q + 1, :]
            to = jnp.where(hits[q] > 0.5, to, -1)
            sel.append(pick(iota((128, 256), 0) == to))
        sel = jnp.concatenate(sel, axis=0)

        def columns(n, carry):
            cols = pl.ds(pl.multiple_of(n * 512, 512), 512)
            out = dot(sel, tok[group * 256 : (group + 1) * 256, cols]).astype(BF)
            g[0, group * 128 : (group + 1) * 128, cols] = out[:128]
            g[1, group * 128 : (group + 1) * 128, cols] = out[128:]
            return carry

        lax.fori_loop(0, D // 512, columns, 0)

    def turn(q):
        row = iota((ROWS, 128), 0) % SLOT
        last = jnp.zeros((ROWS, 128), F32)
        for j in range(3):
            moved = pltpu.roll(got[q, :, j * 128 : (j + 1) * 128].astype(F32), ROWS - 12 + 4 * j, 0)
            last = jnp.where(row // 4 == j, moved, last)
        for j in range(2):
            ht[q, j * 256 : (j + 1) * 256, :] = got[q, :, j * 256 : (j + 1) * 256].T
        ht[q, 512:640, :] = got[q, :, 512:640].T
        ht[q, 640:768, :] = last.astype(BF).T

    def outer(q):
        def columns(n, carry):
            cols = pl.ds(pl.multiple_of(n * 256, 256), 256)
            part[q, :, cols] = dot(ht[q], g[q, :, cols]).astype(BF)
            return carry

        lax.fori_loop(0, D // 256, columns, 0)

    def wait_hid():
        remote(
            got.at[:, pl.ds(SLOT, ROWS - SLOT)], got.at[:, pl.ds(SLOT, ROWS - SLOT)], hid_s, hid_r, partner
        ).wait_recv()

    pieces = [
        lambda: forwards(1, 16),
        lambda: (wait_meta(), gather(0), gather(1)),
        lambda: (wait_hid(), turn(0), turn(1)),
        lambda: (wait_partner(), gather(2), gather(3)),
        lambda: outer(0),
        lambda: outer(1),
    ]
    for i, piece in enumerate(pieces):
        for n in range(PER):
            relay(FIRST + i * PER + n)
        piece()

    def mine(zd):
        return (zd // 4) % 2 == c

    def own(zd, k):
        return (zd // 4) // 2, pl.ds(pl.multiple_of((zd % 4) * SLAB + k * SR, SR), SR)

    def sub(k):
        return pl.ds(pl.multiple_of(k * SR, SR), SR)

    def hop(src, way, s, k):
        land, sem, to = (land_p, rs_rp, up) if way == 0 else (land_m, rs_rm, down)
        return remote(src, land.at[s, sub(k)], rs_s.at[way, s, k], sem.at[s, k], column(to))

    targets = ((0, lambda s: (z + 8 - s) % 16), (1, lambda s: (z + 8 + s) % 16))

    def far(way, k):
        return k >= HALF if way == 0 else k < HALF

    def launch(k, carry):
        for way, target in targets:
            for s in range(2):
                zd = target(s)

                @pl.when(mine(zd) & (far(way, k) if s == 0 else jnp.logical_not(far(way, k))))
                def _():
                    q, rows = own(zd, k)
                    hop(part.at[q, rows], way, s, k).start()

        return carry

    lax.fori_loop(0, SUB, launch, 0)
    def add_sub(n):
        s, k = 1 + n // SUB, n % SUB
        for way, target in targets:
            zd = target(s)
            land = land_p if way == 0 else land_m

            @pl.when(mine(zd) & (far(way, k) | (s > 1)))
            def _():
                q, rows = own(zd, k)
                hop(land.at[s - 1, sub(k)], way, s - 1, k).wait_recv()
                land[s - 1, sub(k), :] = (
                    land[s - 1, sub(k), :].astype(F32) + part[q, rows, :].astype(F32)
                ).astype(BF)
                hop(land.at[s - 1, sub(k)], way, s, k).start()

    def adds(lo, hi):
        def body(n, carry):
            add_sub(n)
            return carry

        lax.fori_loop(lo, hi, body, 0)

    last = FIRST + len(pieces) * PER

    def both(i, carry):
        relay(i)
        for r in range(RATE):
            add_sub((i - last) * RATE + r)
        return carry

    lax.fori_loop(last, STEPS, both, 0)
    done = (STEPS - last) * RATE

    def project(q, tile):
        out = dot(g[q], wbuf[q, tile * 256 : (tile + 1) * 256, :], ((1,), (1,)))
        row = iota((ROWS, 128), 0) % SLOT
        if tile == 2:
            proj5[...] = out[:, 128:]
            cell[q, :, 512:640] = out[:, :128].astype(BF)
            return
        for n in range(2):
            j = tile * 2 + n
            part_out = out[:, n * 128 : (n + 1) * 128]
            if j < 3:
                part_out = jnp.where(row >= 12, pltpu.roll(proj5[...], 12 - 4 * j, 0), part_out)
            cell[q, :, j * 128 : (j + 1) * 128] = part_out.astype(BF)

    def send_back():
        def start(j, carry):
            remote(cell.at[:, slot_rows(j)], back.at[:, slot_rows(j)], ret_s, ret_r, plane(j, -1)).start()
            return carry

        lax.fori_loop(1, PEERS, start, 0)
        back[:, :SLOT, :] = cell[:, :SLOT, :]

    def finish():
        remote(
            back.at[:, pl.ds(SLOT, ROWS - SLOT)], back.at[:, pl.ds(SLOT, ROWS - SLOT)], ret_s, ret_r, partner
        ).wait_recv()
        gate = gcol_ref[:, :1]
        total = jnp.zeros((ROUTES, 1), F32)

        def routed(sel, cols):
            return dot(colsel[sel, :, :ROWS], back[0, :, cols]) + dot(colsel[sel, :, ROWS:], back[1, :, cols])

        for lo, hi in ((0, 256), (256, 512), (512, 640), (640, 768)):
            if lo < CUT:
                out = routed(0, slice(lo, hi))
            else:
                out = sum(routed(1 + j, slice(j * 128, (j + 1) * 128)) for j in range(3))
            hg_ref[:, lo:hi] = (gate * out).astype(BF)
            total += jnp.sum(out * hid_ref[:, lo:hi].astype(F32), axis=1, keepdims=True)
        spread = jnp.where(iota((ROUTES, TOK), 0) // TOP == iota((ROUTES, TOK), 1), total, 0.0)
        gg_ref[...] = jnp.sum(spread.reshape(TOK, TOP, TOK), axis=0)

    marks = [done, done + SUB, done + 2 * SUB, 5 * SUB, 7 * SUB]
    adds(marks[0], marks[1])
    for tile in (2, 0, 1):
        project(0, tile)
    adds(marks[1], marks[2])
    for tile in (2, 0, 1):
        project(1, tile)
    send_back()
    adds(marks[2], marks[3])
    finish()
    adds(marks[3], marks[4])

    @pl.when(mine(z))
    def _():
        def close(n, carry):
            k = n
            kept = n // HALF == c
            q, rows = own(z, k)
            hop(land_p.at[7, sub(k)], 0, 7, k).wait_recv()
            hop(land_m.at[7, sub(k)], 1, 7, k).wait_recv()
            out = (
                land_p[7, sub(k), :].astype(F32)
                + land_m[7, sub(k), :].astype(F32)
                + part[q, rows, :].astype(F32)
            )

            @pl.when(jnp.logical_not(kept))
            def _():
                fin_out[sub(n % HALF), :] = out.astype(BF)
                remote(fin_out.at[sub(n % HALF)], fin_in.at[sub(n % HALF)], fin_s.at[n % HALF], fin_r.at[n % HALF], partner).start()

            @pl.when(kept)
            def _():
                wg_ref[sub(n % HALF), :] = out

            return carry

        lax.fori_loop(0, SUB, close, 0)

        def sent(n, carry):
            remote(fin_out.at[sub(n)], fin_in.at[sub(n)], fin_s.at[n], fin_r.at[n], partner).wait_send()
            return carry

        lax.fori_loop(0, HALF, sent, 0)

    @pl.when(jnp.logical_not(mine(z)))
    def _():
        def close(n, carry):
            remote(fin_out.at[sub(n)], fin_in.at[sub(n)], fin_s.at[n], fin_r.at[n], partner).wait_recv()
            wg_ref[sub(n), :] = fin_in[sub(n), :].astype(F32)
            return carry

        lax.fori_loop(0, HALF, close, 0)

    remote(meta.at[pl.ds(1, PEERS - 1)], meta.at[pl.ds(1, PEERS - 1)], meta_s, meta_r, partner).wait_send()
    remote(tok.at[pl.ds(0, 16 * TOK)], tok.at[pl.ds(0, 16 * TOK)], tok_s, fwd_r, partner).wait_send()
    remote(tok.at[pl.ds(TOK, 15 * TOK)], tok.at[pl.ds(TOK, 15 * TOK)], fwd_s, fwd_r, partner).wait_send()
    remote(
        pack.at[:, pl.ds(SLOT, ROWS - SLOT)], got.at[:, pl.ds(SLOT, ROWS - SLOT)], hid_s, hid_r, partner
    ).wait_send()
    remote(
        cell.at[:, pl.ds(SLOT, ROWS - SLOT)], back.at[:, pl.ds(SLOT, ROWS - SLOT)], ret_s, ret_r, partner
    ).wait_send()

    def all_relayed(i, carry):
        relay_sent(i)
        return carry

    lax.fori_loop(0, CH, all_relayed, 0)

    def all_added(k, carry):
        for way, target in targets:
            for s in range(8):

                @pl.when(mine(target(s)) & (far(way, k) | (s > 0)))
                def _():
                    hop(land_m.at[0, sub(k)], way, s, k).wait_send()

        return carry

    lax.fori_loop(0, SUB, all_added, 0)


def settle(*refs):
    held, sems = refs[6:9], refs[9]
    into = [pltpu.make_async_copy(refs[i], held[i], sems.at[0, i]) for i in range(3)]
    out = [pltpu.make_async_copy(held[i], refs[3 + i], sems.at[1, i]) for i in range(3)]
    for copy in into:
        copy.start()
    for i in range(3):
        into[i].wait()
        out[i].start()
    for copy in out:
        copy.wait()


def on_device(grad_out, hidden, gates, routes, weights):
    tokens, picks = routes.shape
    vmem = pl.BlockSpec(memory_space=pltpu.VMEM)
    dma = pltpu.SemaphoreType.DMA
    results = pl.pallas_call(
        kernel,
        out_shape=(
            jax.ShapeDtypeStruct((ROUTES, F), BF),
            jax.ShapeDtypeStruct((TOP, TOK), F32),
            jax.ShapeDtypeStruct((F // 8, D), F32),
        ),
        in_specs=[vmem, vmem, vmem, vmem, pl.BlockSpec(memory_space=pl.ANY)],
        out_specs=(vmem, vmem, vmem),
        scratch_shapes=[
            pltpu.VMEM((PEERS * TOK, D), BF),
            pltpu.VMEM((PEERS, 16, 128), BF),
            pltpu.VMEM((4, 16, 128), BF),
            pltpu.VMEM((2, ROWS, CUT), BF),
            pltpu.VMEM((2, ROWS, CUT), BF),
            pltpu.VMEM((2, ROWS, CUT), BF),
            pltpu.VMEM((2, ROWS, CUT), BF),
            pltpu.VMEM((4, 2 * ROWS, ROUTES), BF),
            pltpu.VMEM((4, ROUTES, 2 * ROWS), BF),
            pltpu.VMEM((ROUTES, 128), F32),
            pltpu.VMEM((2, F, D), BF),
            pltpu.VMEM((2, ROWS, D), BF),
            pltpu.VMEM((2, F, ROWS), BF),
            pltpu.VMEM((ROWS, 128), F32),
            pltpu.VMEM((2, F, D), BF),
            pltpu.VMEM((8, SLAB, D), BF),
            pltpu.VMEM((8, SLAB, D), BF),
            pltpu.VMEM((F // 8, D), BF),
            pltpu.VMEM((F // 8, D), BF),
            dma, dma, dma, dma, dma((16,)), dma, dma, dma, dma, dma, dma,
            dma((2, CH)), dma((2, CH)), dma((2, 8, SUB)), dma((8, SUB)), dma((8, SUB)),
            dma((HALF,)), dma((HALF,)),
        ],
        compiler_params=pltpu.CompilerParams(
            collective_id=0, has_side_effects=True, vmem_limit_bytes=60 * 2**20
        ),
        cost_estimate=pl.CostEstimate(flops=10**10, bytes_accessed=10**7, transcendentals=0),
        name="routed_down_backward",
    )(routes.T, gates.T, grad_out, hidden.reshape(ROUTES, F), weights.reshape(F, D))
    anywhere = pl.BlockSpec(memory_space=pl.ANY)
    hidden_grad, gate_grad, weight_grad = pl.pallas_call(
        settle,
        out_shape=tuple(jax.ShapeDtypeStruct(r.shape, r.dtype) for r in results),
        in_specs=[anywhere] * 3,
        out_specs=(anywhere,) * 3,
        scratch_shapes=[*(pltpu.VMEM(r.shape, r.dtype) for r in results), dma((2, 3))],
        name="settle_results",
    )(*results)
    return (
        hidden_grad.reshape(tokens, picks, F),
        gate_grad.T,
        weight_grad.reshape(1, F // 8, D),
    )


def solution(mesh):
    return jax.shard_map(
        on_device,
        mesh=mesh,
        in_specs=(
            P(("dp", "expert"), None),
            P(("dp", "expert"), None, None),
            P(("dp", "expert"), None),
            P(("dp", "expert"), None),
            P("expert", None, None),
        ),
        out_specs=(
            P(("dp", "expert"), None, None),
            P(("dp", "expert"), None),
            P("expert", "dp", None),
        ),
        check_vma=False,
    )
```
